768 devices in a mesh: crop: 96 (over z, y_lo, core), branch: 2 (over y_hi), dap: 4 (over x).
Axes of the slice: x: 4, y: 8 (y_hi: 2, y_lo: 4; y = y_hi * 4 + y_lo), z: 12, core: 2. Of those that a mesh axis runs over, the one named last changes fastest.
Arguments:
- homolog_matrix: bfloat16 [6144, 128, 256], P(('crop', 'dap')), parts along dimension 0, may hold values from -6 to 6
- homolog_entry_flags: int32 [6144, 128], P(('crop', 'dap')), parts along dimension 0, may hold values 0 or 1
- couple_matrix: bfloat16 [12288, 128, 128], P(('crop', 'dap')), parts along dimension 0, may hold values from -6 to 6
- window_amino_flags: int32 [12288], P('crop'), parts along dimension 0, may hold values from 0 to 1, as said below
- pairwise_standardize_scaling: float32 [256], replicated, may hold values from 0.1 to 1.9
- pairwise_standardize_offset: float32 [256], replicated, may hold values from -3 to 3
- pairwise_factor_matrices: bfloat16 [256, 64], replicated, may hold values from -0.375 to 0.375
- pairwise_final_matrix: bfloat16 [1024, 128], replicated, may hold values from -0.75 to 0.75
- pairwise_final_offset: float32 [128], replicated, may hold values from -3 to 3
- trimul_entry_standardize_scaling: float32 [128], replicated, may hold values from 0.1 to 1.9
- trimul_entry_standardize_offset: float32 [128], replicated, may hold values from -3 to 3
- trimul_entry_matrices: bfloat16 [128, 640], replicated, may hold values from -0.5 to 0.5
- trimul_entry_offsets: float32 [640], replicated, may hold values from -3 to 3
- trimul_final_standardize_scaling: float32 [128], replicated, may hold values from 0.1 to 1.9
- trimul_final_standardize_offset: float32 [128], replicated, may hold values from -3 to 3
- trimul_final_matrix: bfloat16 [128, 128], replicated, may hold values from -0.5 to 0.5
- trimul_final_offset: float32 [128], replicated, may hold values from -3 to 3
Outputs:
- pair_out: bfloat16 [12288, 128, 128], P(('crop', 'dap'), 'branch'), parts along dimension 0
The draws below stay inside these ranges and needn't reach their ends.
There are 96 independent parts, one for each index of `crop`. The reference program is written for one: setup_inputs(seed, part) draws one part's arguments, and reference() takes and returns one part's arrays. A program takes and returns all parts, laid end to end along the dimension named above; an argument that names none is the same for every part. Nothing has to cross between parts.
Inputs may be any that keep to these rules, and one draw needn't show every extreme that they name: `window_amino_flags`: 1 on the first residues of the crop and 0 on the rest, with at least 64 ones.
All inputs are finite; a program needn't handle non-finite values. No bound on the sum of `homolog_entry_flags` on one device may be relied on, other than what follows from the above.
Results may differ from the reference program's by a relative error of at most 0.0057.
Values may be sent and summed in bfloat16 or wider, within the bound.
No kernel may reach another device: no remote copies, remote signals or barrier semaphores. Data moves between devices by JAX's collectives and lax.ppermute only.
A program may use at most 64 MiB of HBM per device.

```python
import jax
import jax.numpy as jnp
from jax import lax

HOMOLOG_FEATURES = 256
CZ = 128
PAIRWISE_FEATURES = 32
TRI_C = 128
WINDOW_AMINOS = 128
WINDOW_HOMOLOGS = 64


def draw_window_amino_flags(key, part):
    length = jax.random.randint(jax.random.fold_in(key, 17), (), WINDOW_AMINOS // 2, WINDOW_AMINOS + 1)
    return (jnp.arange(WINDOW_AMINOS) < length).astype(jnp.int32)


def place_ends(entries, key, low, high):
    longest = entries.shape.index(max(entries.shape))
    spots = []
    for shift in (0, 1):
        where = [jax.random.randint(jax.random.fold_in(key, axis), (), 0, length) for axis, length in enumerate(entries.shape)]
        where[longest] = (where[longest] + shift) % entries.shape[longest]
        spots.append(tuple(where))
    return entries.at[spots[0]].set(low).at[spots[1]].set(high)


def shard_levels(key, dims, cuts, low, top_value):
    def one(axis_at, shards_of):
        steps = jax.random.uniform(jax.random.fold_in(jax.random.fold_in(key, 6), axis_at), (shards_of,), jnp.float32, low / len(cuts), top_value / len(cuts))
        return jnp.repeat(jnp.exp(steps), dims[axis_at] // shards_of).reshape((-1,) + (1,) * (len(dims) - axis_at - 1))

    level = one(*cuts[0])
    for cut in cuts[1:]:
        level = level * one(*cut)
    return level


def gaussian(own_key, dims, deviation, reach, split=(), kind=jnp.bfloat16):
    array = jax.random.normal(own_key, dims, jnp.float32) * deviation
    if len(split) > 0:
        array = shard_levels(own_key, dims, split, -0.22, 0.18) * array
    return jnp.clip(array, min=-reach, max=reach).astype(kind)


def setup_inputs(seed: int = 0, part: int = 0) -> dict:
    keys = jax.random.split(jax.random.key(seed), 18)
    part_splits = jax.random.split(jax.random.fold_in(keys[17], part), 18)
    homolog_matrix = gaussian(part_splits[0], (WINDOW_HOMOLOGS, WINDOW_AMINOS, HOMOLOG_FEATURES), 1.0, 6.0, ((0, 4),))
    homolog_entry_flags = place_ends((jax.random.randint(part_splits[1], (WINDOW_HOMOLOGS, WINDOW_AMINOS), 0, 4) < 3).astype(jnp.int32), jax.random.fold_in(part_splits[1], 1), 0, 1)
    couple_matrix = gaussian(part_splits[2], (WINDOW_AMINOS, WINDOW_AMINOS, CZ), 1.0, 6.0, ((0, 4),))
    window_amino_flags = draw_window_amino_flags(jax.random.fold_in(jax.random.fold_in(keys[17], part), 71), part)
    pairwise_standardize_scaling = jnp.clip(1.0 + 0.18 * jax.random.normal(keys[4], (HOMOLOG_FEATURES,), jnp.float32), 0.1, 1.9)
    pairwise_standardize_offset = gaussian(keys[5], (HOMOLOG_FEATURES,), 0.5, 3.0, (), jnp.float32)
    pairwise_factor_matrices = gaussian(keys[6], (HOMOLOG_FEATURES, 2 * PAIRWISE_FEATURES), HOMOLOG_FEATURES ** -0.5, 0.375)
    pairwise_final_matrix = gaussian(keys[7], (PAIRWISE_FEATURES * PAIRWISE_FEATURES, CZ), (PAIRWISE_FEATURES * PAIRWISE_FEATURES // 16) ** -0.5, 0.75)
    pairwise_final_offset = gaussian(keys[8], (CZ,), 0.5, 3.0, (), jnp.float32)
    trimul_entry_standardize_scaling = jnp.clip(1.0 + 0.18 * jax.random.normal(keys[9], (CZ,), jnp.float32), 0.1, 1.9)
    trimul_entry_standardize_offset = gaussian(keys[10], (CZ,), 0.5, 3.0, (), jnp.float32)
    trimul_entry_matrices = gaussian(keys[11], (CZ, 4 * TRI_C + CZ), CZ ** -0.5, 0.5)
    trimul_entry_offsets = gaussian(keys[12], (4 * TRI_C + CZ,), 0.5, 3.0, (), jnp.float32)
    trimul_final_standardize_scaling = jnp.clip(1.0 + 0.18 * jax.random.normal(keys[13], (TRI_C,), jnp.float32), 0.1, 1.9)
    trimul_final_standardize_offset = gaussian(keys[14], (TRI_C,), 0.5, 3.0, (), jnp.float32)
    trimul_final_matrix = gaussian(keys[15], (TRI_C, CZ), TRI_C ** -0.5, 0.5)
    trimul_final_offset = gaussian(keys[16], (CZ,), 0.5, 3.0, (), jnp.float32)
    return dict(homolog_matrix=homolog_matrix, homolog_entry_flags=homolog_entry_flags, couple_matrix=couple_matrix, window_amino_flags=window_amino_flags, pairwise_standardize_scaling=pairwise_standardize_scaling, pairwise_standardize_offset=pairwise_standardize_offset, pairwise_factor_matrices=pairwise_factor_matrices, pairwise_final_matrix=pairwise_final_matrix, pairwise_final_offset=pairwise_final_offset, trimul_entry_standardize_scaling=trimul_entry_standardize_scaling, trimul_entry_standardize_offset=trimul_entry_standardize_offset, trimul_entry_matrices=trimul_entry_matrices, trimul_entry_offsets=trimul_entry_offsets, trimul_final_standardize_scaling=trimul_final_standardize_scaling, trimul_final_standardize_offset=trimul_final_standardize_offset, trimul_final_matrix=trimul_final_matrix, trimul_final_offset=trimul_final_offset)


def standardize_features(values, gain_vec, bias_vec):
    center = lax.optimization_barrier(jnp.mean(values, axis=-1, keepdims=True))
    rotated_partner_block = values - center
    spread = lax.optimization_barrier(jnp.mean(rotated_partner_block * rotated_partner_block, axis=-1, keepdims=True))
    return rotated_partner_block * lax.rsqrt(spread + 1e-05) * gain_vec + bias_vec

def reference(homolog_matrix, homolog_entry_flags, couple_matrix, window_amino_flags, pairwise_standardize_scaling, pairwise_standardize_offset, pairwise_factor_matrices, pairwise_final_matrix, pairwise_final_offset, trimul_entry_standardize_scaling, trimul_entry_standardize_offset, trimul_entry_matrices, trimul_entry_offsets, trimul_final_standardize_scaling, trimul_final_standardize_offset, trimul_final_matrix, trimul_final_offset):
    residue_present = window_amino_flags.astype(jnp.float32)
    sequence_present = homolog_entry_flags.astype(jnp.float32) * residue_present[None, :]
    homolog_standardized = standardize_features(homolog_matrix.astype(jnp.float32), pairwise_standardize_scaling, pairwise_standardize_offset).astype(jnp.bfloat16)
    mapped_features = jnp.dot(homolog_standardized.reshape(WINDOW_HOMOLOGS * WINDOW_AMINOS, HOMOLOG_FEATURES), pairwise_factor_matrices, preferred_element_type=jnp.float32)
    mapped_features = mapped_features.reshape(WINDOW_HOMOLOGS, WINDOW_AMINOS, 2 * PAIRWISE_FEATURES) * sequence_present[:, :, None]
    outer_product_left_factor = mapped_features[:, :, :PAIRWISE_FEATURES].astype(jnp.bfloat16)
    outer_product_right_factor = mapped_features[:, :, PAIRWISE_FEATURES:].astype(jnp.bfloat16)
    count = jnp.dot(sequence_present.T, sequence_present, precision=lax.Precision.HIGHEST)
    inverse = 1.0 / jnp.maximum(count, 1.0)
    block_rows = 4 if WINDOW_AMINOS % 4 == 0 else 1
    blocks = WINDOW_AMINOS // block_rows
    left_blocks = jnp.transpose(outer_product_left_factor.reshape(WINDOW_HOMOLOGS, blocks, block_rows, PAIRWISE_FEATURES), (1, 0, 2, 3))
    inverse_blocks = inverse.reshape(blocks, block_rows, WINDOW_AMINOS)
    right_wide = outer_product_right_factor.astype(jnp.float32)

    def one_block(inputs):
        left_block, inverse_block = inputs
        products = jnp.einsum('sic,sjd->ijcd', left_block.astype(jnp.float32), right_wide)
        averaged = (products * inverse_block[:, :, None, None]).astype(jnp.bfloat16)
        flat = averaged.reshape(block_rows * WINDOW_AMINOS, PAIRWISE_FEATURES * PAIRWISE_FEATURES)
        update = jnp.dot(flat, pairwise_final_matrix, preferred_element_type=jnp.float32) + pairwise_final_offset
        return update.reshape(block_rows, WINDOW_AMINOS, CZ).astype(jnp.bfloat16)
    opm_update = lax.map(one_block, (left_blocks, inverse_blocks)).reshape(WINDOW_AMINOS, WINDOW_AMINOS, CZ)
    pair_normed = standardize_features(couple_matrix.astype(jnp.float32), trimul_entry_standardize_scaling, trimul_entry_standardize_offset).astype(jnp.bfloat16)
    tri_projected = jnp.dot(pair_normed.reshape(WINDOW_AMINOS * WINDOW_AMINOS, CZ), trimul_entry_matrices, preferred_element_type=jnp.float32) + trimul_entry_offsets
    tri_projected = tri_projected.reshape(WINDOW_AMINOS, WINDOW_AMINOS, 4 * TRI_C + CZ)
    pair_live = (residue_present[:, None] * residue_present[None, :])[:, :, None]
    tri_left = (jax.nn.sigmoid(tri_projected[:, :, :TRI_C]) * tri_projected[:, :, TRI_C:2 * TRI_C] * pair_live).astype(jnp.bfloat16)
    tri_right = (jax.nn.sigmoid(tri_projected[:, :, 2 * TRI_C:3 * TRI_C]) * tri_projected[:, :, 3 * TRI_C:4 * TRI_C] * pair_live).astype(jnp.bfloat16)
    out_gate = jax.nn.sigmoid(tri_projected[:, :, 4 * TRI_C:])
    tri_sum = jnp.einsum('ikc,jkc->ijc', tri_left.astype(jnp.float32), tri_right.astype(jnp.float32))
    tri_mid = standardize_features(tri_sum, trimul_final_standardize_scaling, trimul_final_standardize_offset).astype(jnp.bfloat16)
    mixed = jnp.dot(tri_mid.reshape(WINDOW_AMINOS * WINDOW_AMINOS, TRI_C), trimul_final_matrix, preferred_element_type=jnp.float32).reshape(WINDOW_AMINOS, WINDOW_AMINOS, CZ)
    tri_update = (out_gate * (mixed + trimul_final_offset)).astype(jnp.bfloat16)
    total = couple_matrix.astype(jnp.float32) + opm_update.astype(jnp.float32) + tri_update.astype(jnp.float32)
    return total.astype(jnp.bfloat16)
```

```python
import jax
import jax.numpy as jnp
from jax import lax
from jax.experimental import pallas as pl
from jax.experimental.pallas import tpu as pltpu
from jax.sharding import PartitionSpec as P

F32 = jnp.float32
BF16 = jnp.bfloat16
EPS = 1e-05
NT = (((1,), (1,)), ((), ()))
VMEM = pl.BlockSpec(memory_space=pltpu.VMEM)
SMEM = pl.BlockSpec(memory_space=pltpu.SMEM)


def dot(a, b):
    return jnp.dot(a, b, preferred_element_type=F32)


def dot_nt(a, b):
    return lax.dot_general(a, b, NT, preferred_element_type=F32)


def sigmoid(v):
    return 0.5 * jnp.tanh(0.5 * v) + 0.5


def flipped(a):
    return jnp.transpose(a.astype(F32))


def column(row, width):
    return jnp.transpose(jnp.broadcast_to(row, (width, row.shape[1])))


def normed(x, gain, bias, ones):
    width = x.shape[1]
    tiles = width // 128
    mean = dot(x, ones[:width])
    mean = mean if tiles == 1 else jnp.concatenate([mean] * tiles, axis=1)
    delta = x.astype(F32) - mean
    square = delta * delta
    high = square.astype(BF16)
    low = (square - high.astype(F32)).astype(BF16)
    spread = dot(jnp.concatenate([high, low], axis=1), ones)
    scale = lax.rsqrt(spread + EPS)
    scale = scale if tiles == 1 else jnp.concatenate([scale] * tiles, axis=1)
    return (delta * scale * gain + bias).astype(BF16)


def msa_kernel(place, x_ref, flag_ref, window_ref, gain_ref, bias_ref, w_ref, *outs):
    d, b = place[0], place[1]
    seqs, residues, width = x_ref.shape
    ones = jnp.full((2 * width, 128), 1.0 / width, BF16)
    wt = flipped(w_ref[...]).astype(BF16)
    gain, bias = gain_ref[...], bias_ref[...]
    live_all = flag_ref[...].astype(F32) * window_ref[...].astype(F32)
    lane = lax.broadcasted_iota(jnp.int32, (8, 128), 1)
    lane16 = lax.broadcasted_iota(jnp.int32, (16, 128), 1)
    first = b == 0

    for s in range(seqs):
        xn = normed(x_ref[s], gain, bias, ones)
        projected = dot_nt(wt, xn)
        live = jnp.broadcast_to(live_all[s : s + 1, :], (8, 128))
        left = [projected[q * 8 : q * 8 + 8] * live for q in range(4)]
        live16 = jnp.concatenate([live, live], axis=0)
        lo = projected[32:48] * live16
        hi = projected[48:64] * live16
        same = jnp.where(lane16 < 64, lo, hi)
        right = jnp.where(
            first,
            jnp.where(lane16 < 64, lo, pltpu.roll(hi, 64, 1)),
            jnp.where(lane16 < 64, pltpu.roll(lo, 64, 1), hi),
        )
        live_cols = jnp.where(first, pltpu.roll(live, 32, 1), pltpu.roll(live, 96, 1))
        for r in range(4):
            dest = lax.rem(d + r, 4)
            merged = jnp.zeros((8, 128), F32)
            for q in range(4):
                turned = pltpu.roll(left[q], lax.rem(32 * (q - dest) + 128, 128), 1)
                merged = jnp.where((lane >= 32 * q) & (lane < 32 * q + 32), turned, merged)
            live_rows = pltpu.roll(live, lax.rem(128 - 32 * dest, 128), 1)
            flags = jnp.where(lane < 32, live_rows, live_cols)
            outs[r][s] = jnp.concatenate([merged, right, flags], axis=0).astype(BF16)


def pair_kernel(
    place, x_ref, window_ref, gain_ref, bias_ref, w_ref, wb_ref, wf_ref,
    left_ref, gate_ref, wcat_ref, scr, xn_scr, wf_scr,
):
    d, b = place[0], place[1]
    rows, residues, width = x_ref.shape
    ones = jnp.full((2 * width, 128), 1.0 / width, BF16)
    gain, bias = gain_ref[...], bias_ref[...]
    wt = flipped(w_ref[:, 0:256]).astype(BF16)
    wg = flipped(w_ref[:, 512:640]).astype(BF16)
    wcol = column(wb_ref[:, 0:256], 128)
    gcol = column(wb_ref[:, 512:640], 128)
    live_k = window_ref[...].astype(F32)

    wf_scr[...] = wf_ref[...].astype(F32)
    for p in range(2):
        for t in range(4):
            parts = [wf_scr[pl.ds(p * 16 + 4 * t + u, 32, stride=32), :] for u in range(4)]
            block = jnp.transpose(jnp.concatenate(parts, axis=0))
            wcat_ref[128 * p : 128 * p + 128, 128 * t : 128 * t + 128] = block.astype(BF16)

    def one(i, _):
        xn = normed(x_ref[i], gain, bias, ones)
        xn_scr[i] = xn
        projected = dot_nt(wt, xn) + wcol
        live = live_k * place[2 + d * rows + i].astype(F32)
        scr[pl.ds(i * 128, 128), :] = sigmoid(projected[0:128]) * projected[128:256] * live
        return 0

    lax.fori_loop(0, rows, one, 0, unroll=4)

    def gates(p, _):
        at = pl.multiple_of(64 * b, 64)
        both = jnp.concatenate(
            [xn_scr[p, pl.ds(at, 64), :], xn_scr[p + rows // 2, pl.ds(at, 64), :]], axis=0
        )
        gate_ref[p] = sigmoid(dot_nt(wg, both) + gcol)
        return 0

    lax.fori_loop(0, rows // 2, gates, 0, unroll=4)

    def turn(c, _):
        left_ref[c] = scr[pl.ds(c, rows, stride=128), :].astype(BF16)
        return 0

    lax.fori_loop(0, 128, turn, 0, unroll=8)


def outer_kernel(m0, m1, m2, m3, wcat_ref, fb_ref, out_ref, m_scr, a_scr, r_scr, inv_scr, s_scr):
    for r, m in enumerate((m0, m1, m2, m3)):
        m_scr[pl.ds(r * 512, 512), :] = m[...].reshape(512, 128).astype(F32)

    def row(k):
        return m_scr[pl.ds(k, 64, stride=32), :]

    flags = row(24)
    count = dot(jnp.transpose(flags).astype(BF16), flags.astype(BF16))[0:32]
    inverse = 1.0 / jnp.maximum(count, 1.0)
    lane = lax.broadcasted_iota(jnp.int32, (16, 128), 1)
    inv_scr[...] = jnp.where(
        lane < 64, pltpu.roll(inverse[0:16], 96, 1), pltpu.roll(inverse[16:32], 32, 1)
    )
    for r in range(8):
        turned = jnp.transpose(row(r))
        for q in range(4):
            a_scr[pl.ds((q * 8 + r) * 32, 32), :] = turned[32 * q : 32 * q + 32]
    for t in range(16):
        r_scr[:, 128 * t : 128 * t + 128] = row(8 + t).astype(BF16)

    wcat = wcat_ref[...]
    bcol = column(fb_ref[...], 128)
    lane2 = lax.broadcasted_iota(jnp.int32, (128, 128), 1)

    def one(p, _):
        a = jnp.concatenate(
            [a_scr[pl.ds(p, 32, stride=32), :], a_scr[pl.ds(p + 16, 32, stride=32), :]], axis=0
        ).astype(BF16)
        products = dot(a, r_scr[...]).astype(BF16)
        stacked = [
            jnp.concatenate(
                [products[0:32, 128 * t : 128 * t + 128], products[32:64, 128 * t : 128 * t + 128]],
                axis=1,
            )
            for t in range(16)
        ]
        update = dot(wcat, jnp.concatenate(stacked, axis=0))
        a0, a1 = update[0:128, 0:128], update[0:128, 128:256]
        b0, b1 = update[128:256, 0:128], update[128:256, 128:256]
        total = jnp.where(lane2 < 64, a0, b1) + pltpu.roll(jnp.where(lane2 < 64, a1, b0), 64, 1)
        out_ref[p] = (total * inv_scr[pl.ds(p, 1), :] + bcol).astype(BF16)
        return 0

    lax.fori_loop(0, 16, one, 0, unroll=2)


def triangle_kernel(
    place, own_ref, far_a, far_b, near_d, window_ref, gain_ref, bias_ref, w_ref, wb_ref,
    left_ref, gate_ref, opm_ref, fg_ref, fo_ref, wt_ref, tb_ref,
    out_ref, r_scr, t_scr,
):
    d, b = place[0], place[1]
    rows, residues, width = own_ref.shape
    member = (d // 2) == b
    ones = jnp.full((2 * width, 128), 1.0 / width, BF16)
    gain, bias = gain_ref[...], bias_ref[...]
    wt = flipped(w_ref[:, 256:512]).astype(BF16)
    wcol = column(wb_ref[:, 256:512], 128)
    live_k = window_ref[...].astype(F32)
    odd = lax.rem(d, 2)

    def project(x, slot, j):
        xn = normed(x, gain, bias, ones)
        projected = dot_nt(wt, xn) + wcol
        at = slot * rows + j
        live = live_k * place[2 + 64 * b + at].astype(F32)
        r_scr[pl.ds(at * 128, 128), :] = sigmoid(projected[0:128]) * projected[128:256] * live

    def one_row(j, _):
        project(jnp.where(member, own_ref[j], near_d[j]), odd, j)
        project(jnp.where(member, far_a[j], far_b[j]), 1 - odd, j)
        return 0

    lax.fori_loop(0, rows, one_row, 0, unroll=2)

    lane = lax.broadcasted_iota(jnp.int32, (16, 128), 1)

    def channel(c, _):
        right = r_scr[pl.ds(c, 64, stride=128), :].astype(BF16)
        prod = dot_nt(left_ref[c], jnp.concatenate([right, right], axis=0))
        t_scr[pl.ds(c * 16, 16), :] = jnp.where(lane < 64, prod[0:16], prod[16:32])
        return 0

    lax.fori_loop(0, 128, channel, 0, unroll=8)

    fg = column(fg_ref[...], 128)
    fo = column(fo_ref[...], 128)
    tb = column(tb_ref[...], 128)
    final = flipped(wt_ref[...]).astype(BF16)

    def finish(p, _):
        x = t_scr[pl.ds(p, 128, stride=16), :]
        mean = jnp.sum(x, axis=0, keepdims=True) * (1.0 / 128)
        delta = x - mean
        spread = jnp.sum(delta * delta, axis=0, keepdims=True) * (1.0 / 128)
        mid = (delta * lax.rsqrt(spread + EPS) * fg + fo).astype(BF16)
        update = (gate_ref[p] * (dot(final, mid) + tb)).astype(BF16)
        total = jnp.transpose(update.astype(F32) + opm_ref[p].astype(F32))
        at = pl.multiple_of(64 * b, 64)
        for h in range(2):
            i = p + h * (rows // 2)
            base = own_ref[i, pl.ds(at, 64), :].astype(F32)
            out_ref[i] = (base + total[64 * h : 64 * h + 64]).astype(BF16)
        return 0

    lax.fori_loop(0, rows // 2, finish, 0, unroll=2)


def call(kernel, shapes, ins, scratch=(), cost=None):
    return pl.pallas_call(
        kernel,
        out_shape=shapes,
        in_specs=ins,
        out_specs=jax.tree.map(lambda _: VMEM, shapes),
        scratch_shapes=list(scratch),
        compiler_params=pltpu.CompilerParams(vmem_limit_bytes=40 * 1024 * 1024),
        cost_estimate=cost,
    )


SDS = jax.ShapeDtypeStruct


def local(
    homolog_matrix,
    homolog_entry_flags,
    couple_matrix,
    window_amino_flags,
    pairwise_standardize_scaling,
    pairwise_standardize_offset,
    pairwise_factor_matrices,
    pairwise_final_matrix,
    pairwise_final_offset,
    trimul_entry_standardize_scaling,
    trimul_entry_standardize_offset,
    trimul_entry_matrices,
    trimul_entry_offsets,
    trimul_final_standardize_scaling,
    trimul_final_standardize_offset,
    trimul_final_matrix,
    trimul_final_offset,
):
    d, b = lax.axis_index("dap"), lax.axis_index("branch")
    rows, residues, width = couple_matrix.shape
    place = jnp.concatenate([jnp.stack([d, b]).astype(jnp.int32), window_amino_flags])
    window = window_amino_flags[None, :]
    both = ("branch", "dap")

    swap = [(0, 1), (1, 0), (7, 6), (6, 7)]
    across = [(0, 3), (1, 2), (7, 4), (6, 5)]
    around = [(4, 2), (5, 3), (3, 5), (2, 4)]
    far_a = lax.ppermute(couple_matrix, both, swap)
    far_b = lax.ppermute(couple_matrix, both, across)
    near_d = lax.ppermute(couple_matrix, both, around)

    seqs = homolog_matrix.shape[0]
    message = SDS((seqs, 32, 128), BF16)
    parts = call(
        msa_kernel, [message] * 4, [SMEM] + [VMEM] * 6,
        cost=pl.CostEstimate(flops=100_000_000, bytes_accessed=2_000_000, transcendentals=0),
    )(
        place, homolog_matrix, homolog_entry_flags, window,
        pairwise_standardize_scaling[None], pairwise_standardize_offset[None],
        pairwise_factor_matrices,
    )
    arrived = [parts[0]] + [
        lax.ppermute(parts[r], "dap", [(k, (k + r) % 4) for k in range(4)]) for r in (1, 2, 3)
    ]

    left, gate, wcat = call(
        pair_kernel,
        [
            SDS((128, rows, 128), BF16),
            SDS((rows // 2, 128, 128), F32),
            SDS((256, 512), BF16),
        ],
        [SMEM] + [VMEM] * 7,
        [
            pltpu.VMEM((rows * 128, 128), F32),
            pltpu.VMEM((rows, 128, 128), BF16),
            pltpu.VMEM((1024, 128), F32),
        ],
        cost=pl.CostEstimate(flops=600_000_000, bytes_accessed=4_000_000, transcendentals=0),
    )(
        place, couple_matrix, window,
        trimul_entry_standardize_scaling[None], trimul_entry_standardize_offset[None],
        trimul_entry_matrices, trimul_entry_offsets[None], pairwise_final_matrix,
    )

    opm = call(
        outer_kernel,
        SDS((rows // 2, 128, 128), BF16),
        [VMEM] * 6,
        [
            pltpu.VMEM((2048, 128), F32),
            pltpu.VMEM((1024, 64), F32),
            pltpu.VMEM((64, 2048), BF16),
            pltpu.VMEM((16, 128), F32),
            pltpu.VMEM((8, 128), F32),
        ],
        cost=pl.CostEstimate(flops=1_600_000_000, bytes_accessed=2_000_000, transcendentals=0),
    )(*arrived, wcat, pairwise_final_offset[None])

    return call(
        triangle_kernel,
        SDS((rows, 64, 128), BF16),
        [SMEM] + [VMEM] * 16,
        [pltpu.VMEM((64 * 128, 128), F32), pltpu.VMEM((128 * 16, 128), F32)],
    )(
        place, couple_matrix, far_a, far_b, near_d, window,
        trimul_entry_standardize_scaling[None], trimul_entry_standardize_offset[None],
        trimul_entry_matrices, trimul_entry_offsets[None],
        left, gate, opm,
        trimul_final_standardize_scaling[None], trimul_final_standardize_offset[None],
        trimul_final_matrix, trimul_final_offset[None],
    )


def solution(mesh):
    placed = (
        P(("crop", "dap"), None, None),
        P(("crop", "dap"), None),
        P(("crop", "dap"), None, None),
        P("crop"),
    ) + (P(),) * 13
    return jax.shard_map(
        local,
        mesh=mesh,
        in_specs=placed,
        out_specs=P(("crop", "dap"), "branch", None),
        check_vma=False,
    )
```

```python
import jax
import jax.numpy as jnp
from jax import lax
from jax.experimental import pallas as pl
from jax.experimental.pallas import tpu as pltpu
from jax.sharding import PartitionSpec as P

F32 = jnp.float32
BF16 = jnp.bfloat16
EPS = 1e-05
NT = (((1,), (1,)), ((), ()))
VMEM = pl.BlockSpec(memory_space=pltpu.VMEM)
SMEM = pl.BlockSpec(memory_space=pltpu.SMEM)
HBM = pl.BlockSpec(memory_space=pltpu.HBM)
ENTRY_MIB = 56
BLOCK = 16
PAIRS = 4


def dot(a, b):
    return jnp.dot(a, b, preferred_element_type=F32)


def dot_nt(a, b):
    return lax.dot_general(a, b, NT, preferred_element_type=F32)


def sigmoid(v):
    return 0.5 * jnp.tanh(0.5 * v) + 0.5


def flipped(a):
    return jnp.transpose(a.astype(F32))


def column(row, width):
    return jnp.transpose(jnp.broadcast_to(row, (width, row.shape[1])))


def centring(width, copies):
    n = width * copies
    r = lax.broadcasted_iota(jnp.int32, (n, n), 0)
    c = lax.broadcasted_iota(jnp.int32, (n, n), 1)
    inside = (r // width) == (c // width)
    value = jnp.where(r == c, 1.0 - 1.0 / width, -1.0 / width)
    return jnp.where(inside, value, 0.0).astype(BF16)


def deviations(blocks, centre, gain, ones):
    n = len(blocks)
    wide = [jnp.concatenate(blocks[i : i + 2], axis=1) for i in range(0, n, 2)]
    delta = dot(jnp.concatenate(wide, axis=0), centre)
    square = (delta * delta).astype(BF16)
    gained = (delta * jnp.concatenate([gain] * 2, axis=1)).astype(BF16)

    def stacked(a):
        parts = [a[64 * i : 64 * i + 128] if i % 2 == 0 else a[64 * i - 64 : 64 * i + 64] for i in range(n)]
        parts = [p[:, 128 * (i % 2) : 128 * (i % 2) + 128] for i, p in enumerate(parts)]
        return jnp.concatenate(parts, axis=0)

    spread = dot_nt(ones, stacked(square))
    return stacked(gained), lax.rsqrt(spread + EPS)[0:1]


def gate_weights(w_ref, wb_ref, bias, at):
    wt = flipped(w_ref[:, at : at + 256])
    shift = jnp.sum(wt * bias, axis=1, keepdims=True)
    col = column(wb_ref[:, at : at + 256], 128) + shift
    half = jnp.where(lax.broadcasted_iota(jnp.int32, (256, 128), 0) < 128, 0.5, 1.0)
    col = col * half
    return (wt * half).astype(BF16), jnp.concatenate([col, col], axis=1)


def gated(wt, col, gained, scale, live):
    projected = dot_nt(wt, gained) * scale + col
    value = projected[128:256] * live
    return jnp.tanh(projected[0:128]) * value + value


def project_rows(x_ref, present, at, rows, live_k, centre, gain, ones, sides):
    def some(u, _):
        i = BLOCK * u
        gained, scale = deviations([x_ref[i + h] for h in range(BLOCK)], centre, gain, ones)
        for v in range(0, BLOCK, 2):
            live = jnp.concatenate(
                [live_k * (0.5 * present[at + i + v + h].astype(F32)) for h in range(2)], axis=1
            )
            lanes = slice(128 * v, 128 * v + 256)
            for wt, col, scr in sides:
                result = gated(wt, col, gained[lanes], scale[:, lanes], live)
                for h in range(2):
                    scr[pl.ds((i + v + h) * 128, 128), :] = result[:, 128 * h : 128 * h + 128]
        return 0

    lax.fori_loop(0, rows // BLOCK, some, 0)


def msa_kernel(x_ref, flag_ref, window_ref, gain_ref, bias_ref, wt_ref, out_ref):
    b = lax.axis_index("branch")
    seqs, residues, width = x_ref.shape
    ones = jnp.full((8, width), 1.0 / width, BF16)
    centre = centring(width, 1)
    wt = wt_ref[...]
    col = jnp.sum(wt.astype(F32) * bias_ref[...], axis=1, keepdims=True)
    live_all = flag_ref[...].astype(F32) * window_ref[...].astype(F32)
    lane = lax.broadcasted_iota(jnp.int32, (8, 128), 1)
    lane16 = lax.broadcasted_iota(jnp.int32, (16, 128), 1)
    first = b == 0

    delta = dot(x_ref[...].reshape(seqs * residues, width), centre)
    spread = dot_nt(ones, (delta * delta).astype(BF16))
    gained = (delta * gain_ref[...]).astype(BF16)
    everything = dot_nt(wt, gained) * lax.rsqrt(spread + EPS)[0:1] + col
    for s in range(seqs):
        live_row = live_all[s : s + 1, :]
        projected = everything[:, 128 * s : 128 * s + 128] * live_row
        live = jnp.broadcast_to(live_row, (8, 128))
        lo, hi = projected[32:48], projected[48:64]
        right = jnp.where(
            first,
            jnp.where(lane16 < 64, lo, pltpu.roll(hi, 64, 1)),
            jnp.where(lane16 < 64, pltpu.roll(lo, 64, 1), hi),
        )
        live_cols = jnp.where(first, pltpu.roll(live, 32, 1), pltpu.roll(live, 96, 1))
        turned = [[projected[q * 8 : q * 8 + 8]] for q in range(4)]
        for q in range(4):
            turned[q] += [pltpu.roll(turned[q][0], 32 * k, 1) for k in range(1, 4)]
        for dest in range(4):
            merged = turned[0][-dest % 4]
            for q in range(1, 4):
                merged = jnp.where(lane >= 32 * q, turned[q][(q - dest) % 4], merged)
            live_rows = pltpu.roll(live, 128 - 32 * dest, 1) if dest else live
            flags = jnp.where(lane < 32, live_rows, live_cols)
            out_ref[dest, s] = jnp.concatenate([merged, right, flags], axis=0).astype(BF16)


def member_of_half():
    return (lax.axis_index("dap") // 2) == lax.axis_index("branch")


def sides_kernel(
    present, couple, window_ref, gain_ref, bias_ref, weight, offset,
    left_ref, right_ref, cross_ref, couple_v, weight_v, left_scr, right_scr, sems,
):
    rows = couple_v.shape[0]
    member = member_of_half()
    copies = [
        pltpu.make_async_copy(src, dst, sems.at[k])
        for k, (src, dst) in enumerate([(weight, weight_v), (couple, couple_v)])
    ]
    for copy in copies:
        copy.start()
    copies[0].wait()
    ones = jnp.full((8, 128), 1.0 / 128, BF16)
    bias = bias_ref[...]
    sides = [
        (*gate_weights(weight_v, offset, bias, 256 * k), scr)
        for k, scr in enumerate((left_scr, right_scr))
    ]
    copies[1].wait()
    live_k = window_ref[...].astype(F32)
    project_rows(
        couple_v, present, lax.axis_index("dap") * rows, rows, live_k,
        centring(128, 2), gain_ref[...], ones, sides,
    )

    def turn(c, _):
        left = [left_scr[pl.ds(c + 64 * h, rows, stride=128), :].astype(BF16) for h in range(2)]
        right = [right_scr[pl.ds(c + 64 * h, rows, stride=128), :].astype(BF16) for h in range(2)]
        for h in range(2):
            left_ref[c + 64 * h] = left[h]
            right_ref[c + 64 * h] = right[h]
        cross_ref[c] = jnp.where(member, right[1], left[0])
        return 0

    lax.fori_loop(0, 64, turn, 0, unroll=8)


def gate_kernel(
    x_ref, gain_ref, bias_ref, w_ref, wb_ref, wf_ref, gate_ref, wcat_ref, wf_scr,
):
    b = lax.axis_index("branch")
    rows = x_ref.shape[0]
    ones = jnp.full((8, 128), 1.0 / 128, BF16)
    centre, gain = centring(128, 2), gain_ref[...]
    wg = flipped(w_ref[:, 512:640])
    gcol = column(wb_ref[:, 512:640], 128) + jnp.sum(wg * bias_ref[...], axis=1, keepdims=True)
    wg, gcol = (0.5 * wg).astype(BF16), 0.5 * gcol
    at = pl.multiple_of(64 * b, 64)

    blocks = [
        jnp.concatenate([x_ref[p, pl.ds(at, 64), :], x_ref[p + rows // 2, pl.ds(at, 64), :]], axis=0)
        for p in range(rows // 2)
    ]
    gained, scale = deviations(blocks, centre, gain, ones)
    projected = dot_nt(wg, gained) * scale
    for p in range(rows // 2):
        part = projected[:, 128 * p : 128 * p + 128] + gcol
        gate_ref[p] = 0.5 * jnp.tanh(part) + 0.5

    wf_scr[...] = wf_ref[...].astype(F32)
    for p in range(2):
        for t in range(4):
            parts = [wf_scr[pl.ds(p * 16 + 4 * t + u, 32, stride=32), :] for u in range(4)]
            block = jnp.transpose(jnp.concatenate(parts, axis=0))
            wcat_ref[128 * p : 128 * p + 128, 128 * t : 128 * t + 128] = block.astype(BF16)


def outer_kernel(m_ref, wcat_ref, fb_ref, out_ref, m_scr, a_scr, r_scr, inv_scr):
    m_scr[...] = m_ref[...].reshape(2048, 128).astype(F32)

    def row(k):
        return m_scr[pl.ds(k, 64, stride=32), :]

    flags = row(24)
    count = dot(jnp.transpose(flags).astype(BF16), flags.astype(BF16))[0:32]
    inverse = 1.0 / jnp.maximum(count, 1.0)
    lane = lax.broadcasted_iota(jnp.int32, (16, 128), 1)
    inv_scr[...] = jnp.where(
        lane < 64, pltpu.roll(inverse[0:16], 96, 1), pltpu.roll(inverse[16:32], 32, 1)
    )
    for r in range(8):
        turned = jnp.transpose(row(r))
        for q in range(4):
            a_scr[pl.ds((q * 8 + r) * 32, 32), :] = turned[32 * q : 32 * q + 32]
    for t in range(16):
        r_scr[:, 128 * t : 128 * t + 128] = row(8 + t).astype(BF16)

    wcat = wcat_ref[...]
    bcol = column(fb_ref[...], 128)
    lane2 = lax.broadcasted_iota(jnp.int32, (128, 128), 1)

    def some(u, _):
        first = PAIRS * u
        a = [a_scr[pl.ds(first + p + 16 * h, 32, stride=32), :] for p in range(PAIRS) for h in range(2)]
        products = dot(jnp.concatenate(a, axis=0).astype(BF16), r_scr[...]).astype(BF16)
        for p in range(PAIRS):
            lo, hi = products[64 * p : 64 * p + 32], products[64 * p + 32 : 64 * p + 64]
            tiles = [slice(128 * t, 128 * t + 128) for t in range(16)]
            stacked = [jnp.concatenate([lo[:, t], hi[:, t]], axis=1) for t in tiles]
            update = dot(wcat, jnp.concatenate(stacked, axis=0))
            a0, a1 = update[0:128, 0:128], update[0:128, 128:256]
            b0, b1 = update[128:256, 0:128], update[128:256, 128:256]
            crossed = pltpu.roll(jnp.where(lane2 < 64, a1, b0), 64, 1)
            total = jnp.where(lane2 < 64, a0, b1) + crossed
            out_ref[first + p] = (total * inv_scr[pl.ds(first + p, 1), :] + bcol).astype(BF16)
        return 0

    lax.fori_loop(0, 16 // PAIRS, some, 0)


def partner_kernel(left_ref, cross_ref, right_ref, swap_ref, own_ref, give_ref):
    even = lax.rem(lax.axis_index("dap"), 2) == 0
    lane = lax.broadcasted_iota(jnp.int32, (16, 128), 1)

    def channel(c, _):
        near, far = right_ref[c], swap_ref[c]
        lo, hi = jnp.where(even, near, far), jnp.where(even, far, near)
        rows = jnp.concatenate([left_ref[c], cross_ref[c]], axis=0)
        prod = dot_nt(rows, jnp.concatenate([lo, hi, lo, hi], axis=0))
        own_ref[pl.ds(c * 16, 16), :] = jnp.where(lane < 64, prod[0:16], prod[16:32])
        give_ref[c] = jnp.where(lane < 64, prod[32:48], prod[48:64]).astype(BF16)
        return 0

    lax.fori_loop(0, 64, channel, 0, unroll=16)


def triangle_kernel(
    own_ref, right_ref, swap_ref, cross_ref, relay_ref, left_ref, sum_ref, taken_ref, gate_ref, opm_ref,
    fg_ref, fo_ref, wt_ref, tb_ref, out_ref, t_scr,
):
    d, b = lax.axis_index("dap"), lax.axis_index("branch")
    rows = own_ref.shape[0]
    member = member_of_half()
    even = lax.rem(d, 2) == 0
    lane = lax.broadcasted_iota(jnp.int32, (16, 128), 1)

    t_scr[0:1024, :] = jnp.where(
        member, sum_ref[...], taken_ref[...].reshape(1024, 128).astype(F32)
    )

    def channel(c, _):
        near = jnp.where(member, right_ref[c + 64], relay_ref[c])
        far = jnp.where(member, swap_ref[c + 64], cross_ref[c])
        lo, hi = jnp.where(even, near, far), jnp.where(even, far, near)
        prod = dot_nt(left_ref[c + 64], jnp.concatenate([lo, hi, lo, hi], axis=0))
        t_scr[pl.ds((c + 64) * 16, 16), :] = jnp.where(lane < 64, prod[0:16], prod[16:32])
        return 0

    lax.fori_loop(0, 64, channel, 0, unroll=16)

    fg = column(fg_ref[...], 128)
    fo = column(fo_ref[...], 128)
    tb = column(tb_ref[...], 128)
    final = flipped(wt_ref[...]).astype(BF16)

    def finish(p, _):
        x = t_scr[pl.ds(p, 128, stride=16), :]
        mean = jnp.sum(x, axis=0, keepdims=True) * (1.0 / 128)
        delta = x - mean
        spread = jnp.sum(delta * delta, axis=0, keepdims=True) * (1.0 / 128)
        mid = (delta * lax.rsqrt(spread + EPS) * fg + fo).astype(BF16)
        update = (gate_ref[p] * (dot(final, mid) + tb)).astype(BF16)
        total = jnp.transpose(update.astype(F32) + opm_ref[p].astype(F32))
        at = pl.multiple_of(64 * b, 64)
        for h in range(2):
            i = p + h * (rows // 2)
            base = own_ref[i, pl.ds(at, 64), :].astype(F32)
            out_ref[i] = (base + total[64 * h : 64 * h + 64]).astype(BF16)
        return 0

    lax.fori_loop(0, rows // 2, finish, 0, unroll=4)


def call(kernel, shapes, ins, scratch=(), flops=0, size=0, mib=20):
    return pl.pallas_call(
        kernel,
        out_shape=shapes,
        in_specs=ins,
        out_specs=jax.tree.map(lambda _: VMEM, shapes),
        scratch_shapes=list(scratch),
        compiler_params=pltpu.CompilerParams(vmem_limit_bytes=mib * 1024 * 1024),
        cost_estimate=pl.CostEstimate(flops=flops, bytes_accessed=size, transcendentals=0),
    )


SDS = jax.ShapeDtypeStruct


def local(
    homolog_matrix,
    homolog_entry_flags,
    couple_matrix,
    window_amino_flags,
    pairwise_standardize_scaling,
    pairwise_standardize_offset,
    pairwise_factor_matrices,
    pairwise_final_matrix,
    pairwise_final_offset,
    trimul_entry_standardize_scaling,
    trimul_entry_standardize_offset,
    trimul_entry_matrices,
    trimul_entry_offsets,
    trimul_final_standardize_scaling,
    trimul_final_standardize_offset,
    trimul_final_matrix,
    trimul_final_offset,
):
    rows, residues, width = couple_matrix.shape
    seqs = homolog_matrix.shape[0]
    window = window_amino_flags[None, :]
    both = ("branch", "dap")
    block = SDS((128, rows, 128), BF16)
    pair_gain = trimul_entry_standardize_scaling[None]
    pair_bias = trimul_entry_standardize_offset[None]
    offsets = trimul_entry_offsets[None]
    scratch = pltpu.VMEM((rows * 128, 128), F32)
    half = SDS((64, rows, 128), BF16)

    left, right, cross = call(
        sides_kernel,
        [block, block, half],
        [SMEM, HBM, VMEM, VMEM, VMEM, HBM, VMEM],
        [
            pltpu.VMEM(couple_matrix.shape, BF16), pltpu.VMEM((128, 640), BF16),
            scratch, scratch, pltpu.SemaphoreType.DMA((2,)),
        ],
        flops=600_000_000, size=4_000_000, mib=ENTRY_MIB,
    )(
        window_amino_flags, couple_matrix, window, pair_gain, pair_bias, trimul_entry_matrices,
        offsets,
    )
    crossed = lax.ppermute(
        cross, both, [(0, 3), (3, 0), (1, 2), (2, 1), (4, 7), (7, 4), (5, 6), (6, 5)]
    )
    swapped = lax.ppermute(right, both, [(0, 1), (1, 0), (7, 6), (6, 7)])

    homolog, cross = lax.optimization_barrier((homolog_matrix, cross))
    message = call(
        msa_kernel, SDS((4, seqs, 32, 128), BF16), [VMEM] * 6,
        flops=100_000_000, size=2_000_000,
    )(
        homolog, homolog_entry_flags, window,
        pairwise_standardize_scaling[None], pairwise_standardize_offset[None],
        pairwise_factor_matrices.T,
    )
    arrived = lax.all_to_all(message, "dap", 0, 0, tiled=True)

    couple, message = lax.optimization_barrier((couple_matrix, message))
    gate, wcat = call(
        gate_kernel,
        [SDS((rows // 2, 128, 128), F32), SDS((256, 512), BF16)],
        [VMEM] * 6,
        [pltpu.VMEM((1024, 128), F32)],
        flops=200_000_000, size=3_000_000,
    )(couple, pair_gain, pair_bias, trimul_entry_matrices, offsets, pairwise_final_matrix)

    relayed = lax.ppermute(crossed, both, [(3, 2), (2, 3), (4, 5), (5, 4)])
    sums, given = call(
        partner_kernel,
        [SDS((1024, 128), F32), SDS((64, 16, 128), BF16)],
        [VMEM] * 4,
        flops=200_000_000, size=3_000_000,
    )(left, crossed, right, swapped)
    taken = lax.ppermute(given, both, [(0, 3), (1, 2), (7, 4), (6, 5)])

    arrived, given = lax.optimization_barrier((arrived, given))
    opm = call(
        outer_kernel,
        SDS((rows // 2, 128, 128), BF16),
        [VMEM] * 3,
        [
            pltpu.VMEM((2048, 128), F32),
            pltpu.VMEM((1024, 64), F32),
            pltpu.VMEM((64, 2048), BF16),
            pltpu.VMEM((16, 128), F32),
        ],
        flops=1_600_000_000, size=2_000_000,
    )(arrived, wcat, pairwise_final_offset[None])

    return call(
        triangle_kernel,
        SDS((rows, 64, 128), BF16),
        [VMEM] * 14,
        [pltpu.VMEM((128 * 16, 128), F32)],
        flops=400_000_000, size=6_000_000,
    )(
        couple_matrix, right, swapped, crossed, relayed, left, sums, taken, gate, opm,
        trimul_final_standardize_scaling[None], trimul_final_standardize_offset[None],
        trimul_final_matrix, trimul_final_offset[None],
    )


def solution(mesh):
    placed = (
        P(("crop", "dap"), None, None),
        P(("crop", "dap"), None),
        P(("crop", "dap"), None, None),
        P("crop"),
    ) + (P(),) * 13
    return jax.shard_map(
        local,
        mesh=mesh,
        in_specs=placed,
        out_specs=P(("crop", "dap"), "branch", None),
        check_vma=False,
    )
```

```python
import jax
import jax.numpy as jnp
from jax import lax
from jax.experimental import pallas as pl
from jax.experimental.pallas import tpu as pltpu
from jax.sharding import PartitionSpec as P

F32 = jnp.float32
BF16 = jnp.bfloat16
EPS = 1e-05
NT = (((1,), (1,)), ((), ()))
VMEM = pl.BlockSpec(memory_space=pltpu.VMEM)
SMEM = pl.BlockSpec(memory_space=pltpu.SMEM)
HBM = pl.BlockSpec(memory_space=pltpu.HBM)
ENTRY_MIB = 56
BLOCK = 32
SIDE_PITCH = 132
SUM_PITCH = 24
MSA_PITCH = 40
PAIRS = 16


def dot(a, b):
    return jnp.dot(a, b, preferred_element_type=F32)


def dot_nt(a, b):
    return lax.dot_general(a, b, NT, preferred_element_type=F32)


def sigmoid(v):
    return 0.5 * jnp.tanh(0.5 * v) + 0.5


def flipped(a):
    return jnp.transpose(a.astype(F32))


def column(row, width):
    return jnp.transpose(jnp.broadcast_to(row, (width, row.shape[1])))


def centring(width, copies):
    n = width * copies
    r = lax.broadcasted_iota(jnp.int32, (n, n), 0)
    c = lax.broadcasted_iota(jnp.int32, (n, n), 1)
    inside = (r // width) == (c // width)
    value = jnp.where(r == c, 1.0 - 1.0 / width, -1.0 / width)
    return jnp.where(inside, value, 0.0).astype(BF16)


def deviations(blocks, centre, gain, ones):
    n = len(blocks)
    wide = [jnp.concatenate(blocks[i : i + 2], axis=1) for i in range(0, n, 2)]
    delta = dot(jnp.concatenate(wide, axis=0), centre)
    square = (delta * delta).astype(BF16)
    gained = (delta * jnp.concatenate([gain] * 2, axis=1)).astype(BF16)

    def stacked(a):
        parts = [a[64 * i : 64 * i + 128] if i % 2 == 0 else a[64 * i - 64 : 64 * i + 64] for i in range(n)]
        parts = [p[:, 128 * (i % 2) : 128 * (i % 2) + 128] for i, p in enumerate(parts)]
        return jnp.concatenate(parts, axis=0)

    spread = dot_nt(ones, stacked(square))
    return stacked(gained), lax.rsqrt(spread + EPS)[0:1]


def gate_weights(w_ref, wb_ref, bias, at):
    wt = flipped(w_ref[:, at : at + 256])
    shift = jnp.sum(wt * bias, axis=1, keepdims=True)
    rows = [wb_ref[k : k + 1, :] for k in (at // 128, at // 128 + 1)]
    col = column(jnp.concatenate(rows, axis=1), 128) + shift
    half = jnp.where(lax.broadcasted_iota(jnp.int32, (256, 128), 0) < 128, 0.5, 1.0)
    col = col * half
    return (wt * half).astype(BF16), jnp.concatenate([col, col], axis=1)


def gated(wt, col, gained, scale, live):
    projected = dot_nt(wt, gained) * scale + col
    value = projected[128:256] * live
    return jnp.tanh(projected[0:128]) * value + value


def project_rows(x_ref, present, at, rows, live_k, centre, gain, ones, sides):
    def some(u, _):
        i = BLOCK * u
        gained, scale = deviations([x_ref[i + h] for h in range(BLOCK)], centre, gain, ones)
        for v in range(0, BLOCK, 2):
            live = jnp.concatenate(
                [live_k * (0.5 * present[at + i + v + h].astype(F32)) for h in range(2)], axis=1
            )
            lanes = slice(128 * v, 128 * v + 256)
            for wt, col, scr in sides:
                result = gated(wt, col, gained[lanes], scale[:, lanes], live)
                for h in range(2):
                    scr[pl.ds((i + v + h) * SIDE_PITCH, 128), :] = result[:, 128 * h : 128 * h + 128]
        return 0

    lax.fori_loop(0, rows // BLOCK, some, 0)


def message_part(b, x_ref, flag_ref, window_ref, gain_ref, bias_ref, wt_ref, out_ref):
    seqs, residues, width = x_ref.shape
    ones = jnp.full((8, width), 1.0 / width, BF16)
    centre = centring(width, 1)
    wt = wt_ref[...]
    col = jnp.sum(wt.astype(F32) * bias_ref[...], axis=1, keepdims=True)
    live_all = flag_ref[...].astype(F32) * window_ref[...].astype(F32)
    lane = lax.broadcasted_iota(jnp.int32, (8, 128), 1)
    lane16 = lax.broadcasted_iota(jnp.int32, (16, 128), 1)
    first = b == 0

    delta = dot(x_ref[...].reshape(seqs * residues, width), centre)
    spread = dot_nt(ones, (delta * delta).astype(BF16))
    gained = (delta * gain_ref[...]).astype(BF16)
    everything = dot_nt(wt, gained) * lax.rsqrt(spread + EPS)[0:1] + col
    for s in range(seqs):
        live_row = live_all[s : s + 1, :]
        projected = everything[:, 128 * s : 128 * s + 128] * live_row
        live = jnp.broadcast_to(live_row, (8, 128))
        lo, hi = projected[32:48], projected[48:64]
        right = jnp.where(
            first,
            jnp.where(lane16 < 64, lo, pltpu.roll(hi, 64, 1)),
            jnp.where(lane16 < 64, pltpu.roll(lo, 64, 1), hi),
        )
        live_cols = jnp.where(first, pltpu.roll(live, 32, 1), pltpu.roll(live, 96, 1))
        turned = [[projected[q * 8 : q * 8 + 8]] for q in range(4)]
        for q in range(4):
            turned[q] += [pltpu.roll(turned[q][0], 32 * k, 1) for k in range(1, 4)]
        for dest in range(4):
            merged = turned[0][-dest % 4]
            for q in range(1, 4):
                merged = jnp.where(lane >= 32 * q, turned[q][(q - dest) % 4], merged)
            live_rows = pltpu.roll(live, 128 - 32 * dest, 1) if dest else live
            flags = jnp.where(lane < 32, live_rows, live_cols)
            out_ref[dest, s] = jnp.concatenate([merged, right, flags], axis=0).astype(BF16)


def member_of_half():
    return (lax.axis_index("dap") // 2) == lax.axis_index("branch")


def sides_kernel(
    present, couple, window_ref, gain_ref, bias_ref, weight, offset,
    left_ref, lower_ref, upper_ref, cross_ref, offset_out,
    couple_v, weight_v, offset_v, left_scr, right_scr, sems,
):
    rows = couple_v.shape[0]
    member = member_of_half()
    copies = [
        pltpu.make_async_copy(src, dst, sems.at[k])
        for k, (src, dst) in enumerate(
            [(weight, weight_v)]
            + [(offset.at[pl.ds(128 * t, 128)], offset_v.at[t]) for t in range(5)]
            + [(couple, couple_v)]
        )
    ]
    for copy in copies:
        copy.start()
    for copy in copies[:-1]:
        copy.wait()
    offset_out[...] = offset_v[...]
    ones = jnp.full((8, 128), 1.0 / 128, BF16)
    bias = bias_ref[...]
    sides = [
        (*gate_weights(weight_v, offset_v, bias, 256 * k), scr)
        for k, scr in enumerate((left_scr, right_scr))
    ]
    copies[-1].wait()
    live_k = window_ref[...].astype(F32)
    project_rows(
        couple_v, present, lax.axis_index("dap") * rows, rows, live_k,
        centring(128, 2), gain_ref[...], ones, sides,
    )

    def turn(c, _):
        left = [left_scr[pl.ds(c + 64 * h, rows, stride=SIDE_PITCH), :].astype(BF16) for h in range(2)]
        right = [right_scr[pl.ds(c + 64 * h, rows, stride=SIDE_PITCH), :].astype(BF16) for h in range(2)]
        for h in range(2):
            left_ref[c + 64 * h] = left[h]
        lower_ref[c], upper_ref[c] = right
        cross_ref[c] = jnp.where(member, right[1], left[0])
        return 0

    lax.fori_loop(0, 64, turn, 0, unroll=8)


def middle_kernel(
    homolog, flag, window, m_gain, m_bias, m_weight,
    x_ref, gain_ref, bias_ref, w_ref, wb_ref, wf_ref, message_ref, gate_ref, wcat_ref, wf_scr,
):
    b = lax.axis_index("branch")
    message_part(b, homolog, flag, window, m_gain, m_bias, m_weight, message_ref)
    rows = x_ref.shape[0]
    ones = jnp.full((8, 128), 1.0 / 128, BF16)
    centre, gain = centring(128, 2), gain_ref[...]
    wg = flipped(w_ref[:, 512:640])
    gcol = column(wb_ref[4:5, :], 128) + jnp.sum(wg * bias_ref[...], axis=1, keepdims=True)
    wg, gcol = (0.5 * wg).astype(BF16), 0.5 * gcol
    at = pl.multiple_of(64 * b, 64)

    blocks = [
        jnp.concatenate([x_ref[p, pl.ds(at, 64), :], x_ref[p + rows // 2, pl.ds(at, 64), :]], axis=0)
        for p in range(rows // 2)
    ]
    gained, scale = deviations(blocks, centre, gain, ones)
    projected = dot_nt(wg, gained) * scale
    for p in range(rows // 2):
        part = projected[:, 128 * p : 128 * p + 128] + gcol
        gate_ref[p] = 0.5 * jnp.tanh(part) + 0.5

    for c in range(32):
        wf_scr[pl.ds(c * MSA_PITCH, 32), :] = wf_ref[pl.ds(c * 32, 32), :].astype(F32)
    for p in range(2):
        for t in range(4):
            parts = [wf_scr[pl.ds(p * 16 + 4 * t + u, 32, stride=MSA_PITCH), :] for u in range(4)]
            block = jnp.transpose(jnp.concatenate(parts, axis=0))
            wcat_ref[128 * p : 128 * p + 128, 128 * t : 128 * t + 128] = block.astype(BF16)


def outer_kernel(m_ref, wcat_ref, fb_ref, out_ref, m_scr, a_scr, r_scr, inv_scr):
    for k in range(64):
        m_scr[pl.ds(k * MSA_PITCH, 32), :] = m_ref[k // 16, k % 16].astype(F32)

    def row(k):
        return m_scr[pl.ds(k, 64, stride=MSA_PITCH), :]

    flags = row(24)
    count = dot(jnp.transpose(flags).astype(BF16), flags.astype(BF16))[0:32]
    inverse = 1.0 / jnp.maximum(count, 1.0)
    lane = lax.broadcasted_iota(jnp.int32, (16, 128), 1)
    inv_scr[...] = jnp.where(
        lane < 64, pltpu.roll(inverse[0:16], 96, 1), pltpu.roll(inverse[16:32], 32, 1)
    )
    for r in range(8):
        turned = jnp.transpose(row(r))
        for q in range(4):
            a_scr[pl.ds((q * 8 + r) * MSA_PITCH, 32), :] = turned[32 * q : 32 * q + 32]
    for t in range(16):
        r_scr[:, 128 * t : 128 * t + 128] = row(8 + t).astype(BF16)

    wcat = wcat_ref[...]
    bcol = column(fb_ref[...], 128)
    lane2 = lax.broadcasted_iota(jnp.int32, (128, 128), 1)

    def some(u, _):
        first = PAIRS * u
        a = [a_scr[pl.ds(first + p + 16 * h, 32, stride=MSA_PITCH), :] for p in range(PAIRS) for h in range(2)]
        products = dot(jnp.concatenate(a, axis=0).astype(BF16), r_scr[...]).astype(BF16)
        for p in range(PAIRS):
            lo, hi = products[64 * p : 64 * p + 32], products[64 * p + 32 : 64 * p + 64]
            tiles = [slice(128 * t, 128 * t + 128) for t in range(16)]
            stacked = [jnp.concatenate([lo[:, t], hi[:, t]], axis=1) for t in tiles]
            update = dot(wcat, jnp.concatenate(stacked, axis=0))
            a0, a1 = update[0:128, 0:128], update[0:128, 128:256]
            b0, b1 = update[128:256, 0:128], update[128:256, 128:256]
            crossed = pltpu.roll(jnp.where(lane2 < 64, a1, b0), 64, 1)
            total = jnp.where(lane2 < 64, a0, b1) + crossed
            out_ref[first + p] = (total * inv_scr[pl.ds(first + p, 1), :] + bcol).astype(BF16)
        return 0

    lax.fori_loop(0, 16 // PAIRS, some, 0)


def partner_kernel(left_ref, cross_ref, right_ref, swap_ref, own_ref, give_ref):
    even = lax.rem(lax.axis_index("dap"), 2) == 0

    def channel(c, _):
        near, far = right_ref[c], swap_ref[c]
        lo, hi = jnp.where(even, near, far), jnp.where(even, far, near)
        rows = jnp.concatenate([left_ref[c], cross_ref[c]], axis=0)
        prod = dot_nt(rows, jnp.concatenate([lo, hi], axis=0))
        own_ref[pl.ds(c * 16, 16), :] = jnp.concatenate([prod[0:16], prod[16:32]], axis=1)
        give_ref[c] = jnp.concatenate([prod[32:48], prod[48:64]], axis=1).astype(BF16)
        return 0

    lax.fori_loop(0, 64, channel, 0, unroll=32)


def triangle_kernel(
    own_ref, right_ref, swap_ref, cross_ref, relay_ref, left_ref, sum_ref, taken_ref, gate_ref, opm_ref,
    fg_ref, fo_ref, wt_ref, tb_ref, out_ref, t_scr,
):
    d, b = lax.axis_index("dap"), lax.axis_index("branch")
    rows = own_ref.shape[0]
    member = member_of_half()
    even = lax.rem(d, 2) == 0

    for c in range(64):
        t_scr[pl.ds(c * SUM_PITCH, 16), :] = jnp.where(
            member, sum_ref[pl.ds(c * 16, 16), :], taken_ref[c].astype(F32)
        )

    def channel(c, _):
        near = jnp.where(member, right_ref[c], relay_ref[c])
        far = jnp.where(member, swap_ref[c], cross_ref[c])
        lo, hi = jnp.where(even, near, far), jnp.where(even, far, near)
        prod = dot_nt(left_ref[c + 64], jnp.concatenate([lo, hi], axis=0))
        sums = jnp.concatenate([prod[0:16], prod[16:32]], axis=1)
        t_scr[pl.ds((c + 64) * SUM_PITCH, 16), :] = sums
        return 0

    lax.fori_loop(0, 64, channel, 0, unroll=32)

    fg = column(fg_ref[...], 128)
    fo = column(fo_ref[...], 128)
    tb = column(tb_ref[...], 128)
    final = flipped(wt_ref[...]).astype(BF16)

    def finish(p, _):
        x = t_scr[pl.ds(p, 128, stride=SUM_PITCH), :]
        mean = jnp.sum(x, axis=0, keepdims=True) * (1.0 / 128)
        delta = x - mean
        spread = jnp.sum(delta * delta, axis=0, keepdims=True) * (1.0 / 128)
        mid = (delta * lax.rsqrt(spread + EPS) * fg + fo).astype(BF16)
        update = (gate_ref[p] * (dot(final, mid) + tb)).astype(BF16)
        total = jnp.transpose(update.astype(F32) + opm_ref[p].astype(F32))
        at = pl.multiple_of(64 * b, 64)
        for h in range(2):
            i = p + h * (rows // 2)
            base = own_ref[i, pl.ds(at, 64), :].astype(F32)
            out_ref[i] = (base + total[64 * h : 64 * h + 64]).astype(BF16)
        return 0

    lax.fori_loop(0, rows // 2, finish, 0, unroll=16)


def call(kernel, shapes, ins, scratch=(), flops=0, size=0, mib=20):
    return pl.pallas_call(
        kernel,
        out_shape=shapes,
        in_specs=ins,
        out_specs=jax.tree.map(lambda _: VMEM, shapes),
        scratch_shapes=list(scratch),
        compiler_params=pltpu.CompilerParams(vmem_limit_bytes=mib * 1024 * 1024),
        cost_estimate=pl.CostEstimate(flops=flops, bytes_accessed=size, transcendentals=0),
    )


SDS = jax.ShapeDtypeStruct


def local(
    homolog_matrix,
    homolog_entry_flags,
    couple_matrix,
    window_amino_flags,
    pairwise_standardize_scaling,
    pairwise_standardize_offset,
    pairwise_factor_matrices,
    pairwise_final_matrix,
    pairwise_final_offset,
    trimul_entry_standardize_scaling,
    trimul_entry_standardize_offset,
    trimul_entry_matrices,
    trimul_entry_offsets,
    trimul_final_standardize_scaling,
    trimul_final_standardize_offset,
    trimul_final_matrix,
    trimul_final_offset,
):
    rows, residues, width = couple_matrix.shape
    seqs = homolog_matrix.shape[0]
    window = window_amino_flags[None, :]
    both = ("branch", "dap")
    block = SDS((128, rows, 128), BF16)
    pair_gain = trimul_entry_standardize_scaling[None]
    pair_bias = trimul_entry_standardize_offset[None]
    scratch = pltpu.VMEM((rows * SIDE_PITCH, 128), F32)
    half = SDS((64, rows, 128), BF16)

    left, lower, upper, cross, offsets = call(
        sides_kernel,
        [block, half, half, half, SDS((8, 128), F32)],
        [SMEM, HBM, VMEM, VMEM, VMEM, HBM, HBM],
        [
            pltpu.VMEM(couple_matrix.shape, BF16), pltpu.VMEM((128, 640), BF16),
            pltpu.VMEM((8, 128), F32), scratch, scratch, pltpu.SemaphoreType.DMA((7,)),
        ],
        flops=600_000_000, size=4_000_000, mib=ENTRY_MIB,
    )(
        window_amino_flags, couple_matrix, window, pair_gain, pair_bias, trimul_entry_matrices,
        trimul_entry_offsets,
    )
    swap = [(0, 1), (1, 0), (7, 6), (6, 7)]
    crossed = lax.ppermute(
        cross, both, [(0, 3), (3, 0), (1, 2), (2, 1), (4, 7), (7, 4), (5, 6), (6, 5)]
    )
    swapped = lax.ppermute(lower, both, swap)

    homolog, cross = lax.optimization_barrier((homolog_matrix, cross))
    message, gate, wcat = call(
        middle_kernel,
        [SDS((4, seqs, 32, 128), BF16), SDS((rows // 2, 128, 128), F32), SDS((256, 512), BF16)],
        [VMEM] * 12,
        [pltpu.VMEM((32 * MSA_PITCH, 128), F32)],
        flops=300_000_000, size=5_000_000, mib=ENTRY_MIB,
    )(
        homolog, homolog_entry_flags, window,
        pairwise_standardize_scaling[None], pairwise_standardize_offset[None],
        pairwise_factor_matrices.T,
        couple_matrix, pair_gain, pair_bias, trimul_entry_matrices, offsets, pairwise_final_matrix,
    )
    arrived = lax.all_to_all(message, "dap", 0, 0, tiled=True)

    crossed, swapped, upper = lax.optimization_barrier((crossed, swapped, upper))
    relayed = lax.ppermute(crossed, both, [(3, 2), (2, 3), (4, 5), (5, 4)])
    swapped_upper = lax.ppermute(upper, both, swap)
    sums, given = call(
        partner_kernel,
        [SDS((1024, 128), F32), SDS((64, 16, 128), BF16)],
        [VMEM] * 4,
        flops=200_000_000, size=3_000_000,
    )(left, crossed, lower, swapped)
    taken = lax.ppermute(given, both, [(0, 3), (1, 2), (7, 4), (6, 5)])

    arrived, given = lax.optimization_barrier((arrived, given))
    opm = call(
        outer_kernel,
        SDS((rows // 2, 128, 128), BF16),
        [VMEM] * 3,
        [
            pltpu.VMEM((64 * MSA_PITCH, 128), F32),
            pltpu.VMEM((32 * MSA_PITCH, 64), F32),
            pltpu.VMEM((64, 2048), BF16),
            pltpu.VMEM((16, 128), F32),
        ],
        flops=1_600_000_000, size=2_000_000,
    )(arrived, wcat, pairwise_final_offset[None])

    return call(
        triangle_kernel,
        SDS((rows, 64, 128), BF16),
        [VMEM] * 14,
        [pltpu.VMEM((128 * SUM_PITCH, 128), F32)],
        flops=400_000_000, size=6_000_000,
    )(
        couple_matrix, upper, swapped_upper, crossed, relayed, left, sums, taken, gate, opm,
        trimul_final_standardize_scaling[None], trimul_final_standardize_offset[None],
        trimul_final_matrix, trimul_final_offset[None],
    )


def solution(mesh):
    placed = (
        P(("crop", "dap"), None, None),
        P(("crop", "dap"), None),
        P(("crop", "dap"), None, None),
        P("crop"),
    ) + (P(),) * 13
    return jax.shard_map(
        local,
        mesh=mesh,
        in_specs=placed,
        out_specs=P(("crop", "dap"), "branch", None),
        check_vma=False,
    )
```

```python
import jax
import jax.numpy as jnp
from jax import lax
from jax.experimental import pallas as pl
from jax.experimental.pallas import tpu as pltpu
from jax.sharding import PartitionSpec as P

F32 = jnp.float32
BF16 = jnp.bfloat16
EPS = 1e-05
NT = (((1,), (1,)), ((), ()))
VMEM = pl.BlockSpec(memory_space=pltpu.VMEM)
SMEM = pl.BlockSpec(memory_space=pltpu.SMEM)
HBM = pl.BlockSpec(memory_space=pltpu.HBM)
ENTRY_MIB = 56
BLOCK = 32
SIDE_PITCH = 132
SUM_PITCH = 24
MSA_PITCH = 40
PAIRS = 16


def dot(a, b):
    return jnp.dot(a, b, preferred_element_type=F32)


def dot_nt(a, b):
    return lax.dot_general(a, b, NT, preferred_element_type=F32)


def sigmoid(v):
    return 0.5 * jnp.tanh(0.5 * v) + 0.5


def flipped(a):
    return jnp.transpose(a.astype(F32))


def column(row, width):
    return jnp.transpose(jnp.broadcast_to(row, (width, row.shape[1])))


def centring(width, copies):
    n = width * copies
    r = lax.broadcasted_iota(jnp.int32, (n, n), 0)
    c = lax.broadcasted_iota(jnp.int32, (n, n), 1)
    inside = (r // width) == (c // width)
    value = jnp.where(r == c, 1.0 - 1.0 / width, -1.0 / width)
    return jnp.where(inside, value, 0.0).astype(BF16)


def deviations(blocks, centre, gain, ones):
    n = len(blocks)
    wide = [jnp.concatenate(blocks[i : i + 2], axis=1) for i in range(0, n, 2)]
    delta = dot(jnp.concatenate(wide, axis=0), centre)
    square = (delta * delta).astype(BF16)
    gained = (delta * jnp.concatenate([gain] * 2, axis=1)).astype(BF16)

    def stacked(a):
        parts = [a[64 * i : 64 * i + 128] if i % 2 == 0 else a[64 * i - 64 : 64 * i + 64] for i in range(n)]
        parts = [p[:, 128 * (i % 2) : 128 * (i % 2) + 128] for i, p in enumerate(parts)]
        return jnp.concatenate(parts, axis=0)

    spread = dot_nt(ones, stacked(square))
    return stacked(gained), lax.rsqrt(spread + EPS)[0:1]


def gate_weights(w_ref, wb_ref, bias, at):
    wt = flipped(w_ref[:, at : at + 256])
    shift = jnp.sum(wt * bias, axis=1, keepdims=True)
    rows = [wb_ref[k : k + 1, :] for k in (at // 128, at // 128 + 1)]
    col = column(jnp.concatenate(rows, axis=1), 128) + shift
    half = jnp.where(lax.broadcasted_iota(jnp.int32, (256, 128), 0) < 128, 0.5, 1.0)
    col = col * half
    return (wt * half).astype(BF16), jnp.concatenate([col, col], axis=1)


def gated(wt, col, gained, scale, live):
    projected = dot_nt(wt, gained) * scale + col
    value = projected[128:256] * live
    return jnp.tanh(projected[0:128]) * value + value


def project_rows(x_ref, present, at, rows, live_k, centre, gain, ones, sides):
    def some(u, _):
        i = BLOCK * u
        gained, scale = deviations([x_ref[i + h] for h in range(BLOCK)], centre, gain, ones)
        for v in range(0, BLOCK, 2):
            live = jnp.concatenate(
                [live_k * (0.5 * present[at + i + v + h].astype(F32)) for h in range(2)], axis=1
            )
            lanes = slice(128 * v, 128 * v + 256)
            for wt, col, scr in sides:
                result = gated(wt, col, gained[lanes], scale[:, lanes], live)
                for h in range(2):
                    scr[pl.ds((i + v + h) * SIDE_PITCH, 128), :] = result[:, 128 * h : 128 * h + 128]
        return 0

    lax.fori_loop(0, rows // BLOCK, some, 0)


def message_part(b, x_ref, flag_ref, window_ref, gain_ref, bias_ref, wt_ref, out_ref):
    seqs, residues, width = x_ref.shape
    ones = jnp.full((8, width), 1.0 / width, BF16)
    centre = centring(width, 1)
    wt = wt_ref[...]
    col = jnp.sum(wt.astype(F32) * bias_ref[...], axis=1, keepdims=True)
    live_all = flag_ref[...].astype(F32) * window_ref[...].astype(F32)
    lane = lax.broadcasted_iota(jnp.int32, (8, 128), 1)
    lane16 = lax.broadcasted_iota(jnp.int32, (16, 128), 1)
    first = b == 0

    delta = dot(x_ref[...].reshape(seqs * residues, width), centre)
    spread = dot_nt(ones, (delta * delta).astype(BF16))
    gained = (delta * gain_ref[...]).astype(BF16)
    everything = dot_nt(wt, gained) * lax.rsqrt(spread + EPS)[0:1] + col
    for s in range(seqs):
        live_row = live_all[s : s + 1, :]
        projected = everything[:, 128 * s : 128 * s + 128] * live_row
        live = jnp.broadcast_to(live_row, (8, 128))
        lo, hi = projected[32:48], projected[48:64]
        right = jnp.where(
            first,
            jnp.where(lane16 < 64, lo, pltpu.roll(hi, 64, 1)),
            jnp.where(lane16 < 64, pltpu.roll(lo, 64, 1), hi),
        )
        live_cols = jnp.where(first, pltpu.roll(live, 32, 1), pltpu.roll(live, 96, 1))
        turned = [[projected[q * 8 : q * 8 + 8]] for q in range(4)]
        for q in range(4):
            turned[q] += [pltpu.roll(turned[q][0], 32 * k, 1) for k in range(1, 4)]
        for dest in range(4):
            merged = turned[0][-dest % 4]
            for q in range(1, 4):
                merged = jnp.where(lane >= 32 * q, turned[q][(q - dest) % 4], merged)
            live_rows = pltpu.roll(live, 128 - 32 * dest, 1) if dest else live
            flags = jnp.where(lane < 32, live_rows, live_cols)
            out_ref[dest, s] = jnp.concatenate([merged, right, flags], axis=0).astype(BF16)


def member_of_half():
    return (lax.axis_index("dap") // 2) == lax.axis_index("branch")


def sides_kernel(
    present, couple, window_ref, gain_ref, bias_ref, weight, offset,
    left_ref, lower_ref, upper_ref, cross_ref, offset_out,
    couple_v, weight_v, offset_v, left_scr, right_scr, sems,
):
    rows = couple_v.shape[0]
    member = member_of_half()
    copies = [
        pltpu.make_async_copy(src, dst, sems.at[k])
        for k, (src, dst) in enumerate(
            [(weight, weight_v)]
            + [(offset.at[pl.ds(128 * t, 128)], offset_v.at[t]) for t in range(5)]
            + [(couple, couple_v)]
        )
    ]
    for copy in copies:
        copy.start()
    for copy in copies[:-1]:
        copy.wait()
    offset_out[...] = offset_v[...]
    ones = jnp.full((8, 128), 1.0 / 128, BF16)
    bias = bias_ref[...]
    sides = [
        (*gate_weights(weight_v, offset_v, bias, 256 * k), scr)
        for k, scr in enumerate((left_scr, right_scr))
    ]
    copies[-1].wait()
    live_k = window_ref[...].astype(F32)
    project_rows(
        couple_v, present, lax.axis_index("dap") * rows, rows, live_k,
        centring(128, 2), gain_ref[...], ones, sides,
    )

    def turn(c, _):
        left = [left_scr[pl.ds(c + 64 * h, rows, stride=SIDE_PITCH), :].astype(BF16) for h in range(2)]
        right = [right_scr[pl.ds(c + 64 * h, rows, stride=SIDE_PITCH), :].astype(BF16) for h in range(2)]
        for h in range(2):
            left_ref[c + 64 * h] = left[h]
        lower_ref[c], upper_ref[c] = right
        cross_ref[c] = jnp.where(member, right[1], left[0])
        return 0

    lax.fori_loop(0, 64, turn, 0, unroll=8)


def middle_kernel(
    homolog, flag, window, m_gain, m_bias, m_weight,
    x_ref, gain_ref, bias_ref, w_ref, wb_ref, wf_ref, message_ref, gate_ref, wcat_ref, wf_scr,
):
    b = lax.axis_index("branch")
    message_part(b, homolog, flag, window, m_gain, m_bias, m_weight, message_ref)
    rows = x_ref.shape[0]
    ones = jnp.full((8, 128), 1.0 / 128, BF16)
    centre, gain = centring(128, 2), gain_ref[...]
    wg = flipped(w_ref[:, 512:640])
    gcol = column(wb_ref[4:5, :], 128) + jnp.sum(wg * bias_ref[...], axis=1, keepdims=True)
    wg, gcol = (0.5 * wg).astype(BF16), 0.5 * gcol
    at = pl.multiple_of(64 * b, 64)

    blocks = [
        jnp.concatenate([x_ref[p, pl.ds(at, 64), :], x_ref[p + rows // 2, pl.ds(at, 64), :]], axis=0)
        for p in range(rows // 2)
    ]
    gained, scale = deviations(blocks, centre, gain, ones)
    projected = dot_nt(wg, gained) * scale
    for p in range(rows // 2):
        part = projected[:, 128 * p : 128 * p + 128] + gcol
        gate_ref[p] = 0.5 * jnp.tanh(part) + 0.5

    for c in range(32):
        wf_scr[pl.ds(c * MSA_PITCH, 32), :] = wf_ref[pl.ds(c * 32, 32), :].astype(F32)
    for p in range(2):
        for t in range(4):
            parts = [wf_scr[pl.ds(p * 16 + 4 * t + u, 32, stride=MSA_PITCH), :] for u in range(4)]
            block = jnp.transpose(jnp.concatenate(parts, axis=0))
            wcat_ref[128 * p : 128 * p + 128, 128 * t : 128 * t + 128] = block.astype(BF16)


def outer_kernel(m_ref, wcat_ref, fb_ref, out_ref, m_scr, a_scr, r_scr, inv_scr):
    for k in range(64):
        m_scr[pl.ds(k * MSA_PITCH, 32), :] = m_ref[k // 16, k % 16].astype(F32)

    def row(k):
        return m_scr[pl.ds(k, 64, stride=MSA_PITCH), :]

    flags = row(24)
    count = dot(jnp.transpose(flags).astype(BF16), flags.astype(BF16))[0:32]
    inverse = 1.0 / jnp.maximum(count, 1.0)
    lane = lax.broadcasted_iota(jnp.int32, (16, 128), 1)
    inv_scr[...] = jnp.where(
        lane < 64, pltpu.roll(inverse[0:16], 96, 1), pltpu.roll(inverse[16:32], 32, 1)
    )
    for r in range(8):
        turned = jnp.transpose(row(r))
        for q in range(4):
            a_scr[pl.ds((q * 8 + r) * MSA_PITCH, 32), :] = turned[32 * q : 32 * q + 32]
    for t in range(16):
        r_scr[:, 128 * t : 128 * t + 128] = row(8 + t).astype(BF16)

    wcat = wcat_ref[...]
    bcol = column(fb_ref[...], 128)
    lane2 = lax.broadcasted_iota(jnp.int32, (128, 128), 1)

    def some(u, _):
        first = PAIRS * u
        a = [a_scr[pl.ds(first + p + 16 * h, 32, stride=MSA_PITCH), :] for p in range(PAIRS) for h in range(2)]
        products = dot(jnp.concatenate(a, axis=0).astype(BF16), r_scr[...]).astype(BF16)
        for p in range(PAIRS):
            lo, hi = products[64 * p : 64 * p + 32], products[64 * p + 32 : 64 * p + 64]
            tiles = [slice(128 * t, 128 * t + 128) for t in range(16)]
            stacked = [jnp.concatenate([lo[:, t], hi[:, t]], axis=1) for t in tiles]
            update = dot(wcat, jnp.concatenate(stacked, axis=0))
            a0, a1 = update[0:128, 0:128], update[0:128, 128:256]
            b0, b1 = update[128:256, 0:128], update[128:256, 128:256]
            crossed = pltpu.roll(jnp.where(lane2 < 64, a1, b0), 64, 1)
            total = jnp.where(lane2 < 64, a0, b1) + crossed
            out_ref[first + p] = (total * inv_scr[pl.ds(first + p, 1), :] + bcol).astype(BF16)
        return 0

    lax.fori_loop(0, 16 // PAIRS, some, 0)


def partner_kernel(left_ref, cross_ref, right_ref, swap_ref, own_ref, give_ref):
    even = lax.rem(lax.axis_index("dap"), 2) == 0

    def channel(c, _):
        near, far = right_ref[c], swap_ref[c]
        lo, hi = jnp.where(even, near, far), jnp.where(even, far, near)
        rows = jnp.concatenate([left_ref[c], cross_ref[c]], axis=0)
        prod = dot_nt(rows, jnp.concatenate([lo, hi], axis=0))
        own_ref[pl.ds(c * 16, 16), :] = jnp.concatenate([prod[0:16], prod[16:32]], axis=1)
        give_ref[c] = jnp.concatenate([prod[32:48], prod[48:64]], axis=1).astype(BF16)
        return 0

    lax.fori_loop(0, 64, channel, 0, unroll=32)


def triangle_kernel(
    own_ref, right_ref, swap_ref, cross_ref, relay_ref, left_ref, sum_ref, taken_ref, gate_ref, opm_ref,
    fg_ref, fo_ref, wt_ref, tb_ref, out_ref, t_scr,
):
    d, b = lax.axis_index("dap"), lax.axis_index("branch")
    rows = own_ref.shape[0]
    member = member_of_half()
    even = lax.rem(d, 2) == 0

    for c in range(64):
        t_scr[pl.ds(c * SUM_PITCH, 16), :] = jnp.where(
            member, sum_ref[pl.ds(c * 16, 16), :], taken_ref[c].astype(F32)
        )

    def channel(c, _):
        near = jnp.where(member, right_ref[c], relay_ref[c])
        far = jnp.where(member, swap_ref[c], cross_ref[c])
        lo, hi = jnp.where(even, near, far), jnp.where(even, far, near)
        prod = dot_nt(left_ref[c + 64], jnp.concatenate([lo, hi], axis=0))
        sums = jnp.concatenate([prod[0:16], prod[16:32]], axis=1)
        t_scr[pl.ds((c + 64) * SUM_PITCH, 16), :] = sums
        return 0

    lax.fori_loop(0, 64, channel, 0, unroll=32)

    fg = column(fg_ref[...], 128)
    fo = column(fo_ref[...], 128)
    tb = column(tb_ref[...], 128)
    final = flipped(wt_ref[...]).astype(BF16)

    def finish(p, _):
        x = t_scr[pl.ds(p, 128, stride=SUM_PITCH), :]
        mean = jnp.sum(x, axis=0, keepdims=True) * (1.0 / 128)
        delta = x - mean
        spread = jnp.sum(delta * delta, axis=0, keepdims=True) * (1.0 / 128)
        mid = (delta * lax.rsqrt(spread + EPS) * fg + fo).astype(BF16)
        update = (gate_ref[p] * (dot(final, mid) + tb)).astype(BF16)
        total = jnp.transpose(update.astype(F32) + opm_ref[p].astype(F32))
        at = pl.multiple_of(64 * b, 64)
        for h in range(2):
            i = p + h * (rows // 2)
            base = own_ref[i, pl.ds(at, 64), :].astype(F32)
            out_ref[i] = (base + total[64 * h : 64 * h + 64]).astype(BF16)
        return 0

    lax.fori_loop(0, rows // 2, finish, 0, unroll=16)


def call(kernel, shapes, ins, scratch=(), flops=0, size=0, mib=20):
    return pl.pallas_call(
        kernel,
        out_shape=shapes,
        in_specs=ins,
        out_specs=jax.tree.map(lambda _: VMEM, shapes),
        scratch_shapes=list(scratch),
        compiler_params=pltpu.CompilerParams(vmem_limit_bytes=mib * 1024 * 1024),
        cost_estimate=pl.CostEstimate(flops=flops, bytes_accessed=size, transcendentals=0),
    )


SDS = jax.ShapeDtypeStruct


def local(
    homolog_matrix,
    homolog_entry_flags,
    couple_matrix,
    window_amino_flags,
    pairwise_standardize_scaling,
    pairwise_standardize_offset,
    pairwise_factor_matrices,
    pairwise_final_matrix,
    pairwise_final_offset,
    trimul_entry_standardize_scaling,
    trimul_entry_standardize_offset,
    trimul_entry_matrices,
    trimul_entry_offsets,
    trimul_final_standardize_scaling,
    trimul_final_standardize_offset,
    trimul_final_matrix,
    trimul_final_offset,
):
    rows, residues, width = couple_matrix.shape
    seqs = homolog_matrix.shape[0]
    window = window_amino_flags[None, :]
    both = ("branch", "dap")
    block = SDS((128, rows, 128), BF16)
    pair_gain = trimul_entry_standardize_scaling[None]
    pair_bias = trimul_entry_standardize_offset[None]
    scratch = pltpu.VMEM((rows * SIDE_PITCH, 128), F32)
    half = SDS((64, rows, 128), BF16)

    left, lower, upper, cross, offsets = call(
        sides_kernel,
        [block, half, half, half, SDS((8, 128), F32)],
        [SMEM, HBM, VMEM, VMEM, VMEM, HBM, HBM],
        [
            pltpu.VMEM(couple_matrix.shape, BF16), pltpu.VMEM((128, 640), BF16),
            pltpu.VMEM((8, 128), F32), scratch, scratch, pltpu.SemaphoreType.DMA((7,)),
        ],
        flops=600_000_000, size=4_000_000, mib=ENTRY_MIB,
    )(
        window_amino_flags, couple_matrix, window, pair_gain, pair_bias, trimul_entry_matrices,
        trimul_entry_offsets,
    )
    swap = [(0, 1), (1, 0), (7, 6), (6, 7)]
    crossed = lax.ppermute(
        cross, both, [(0, 3), (3, 0), (1, 2), (2, 1), (4, 7), (7, 4), (5, 6), (6, 5)]
    )
    swapped = lax.ppermute(lower, both, swap)

    homolog, cross = lax.optimization_barrier((homolog_matrix, cross))
    message, gate, wcat = call(
        middle_kernel,
        [SDS((4, seqs, 32, 128), BF16), SDS((rows // 2, 128, 128), F32), SDS((256, 512), BF16)],
        [VMEM] * 12,
        [pltpu.VMEM((32 * MSA_PITCH, 128), F32)],
        flops=300_000_000, size=5_000_000, mib=ENTRY_MIB,
    )(
        homolog, homolog_entry_flags, window,
        pairwise_standardize_scaling[None], pairwise_standardize_offset[None],
        pairwise_factor_matrices.T,
        couple_matrix, pair_gain, pair_bias, trimul_entry_matrices, offsets, pairwise_final_matrix,
    )
    arrived = lax.all_to_all(message, "dap", 0, 0, tiled=True)
    upper, gate = lax.optimization_barrier((upper, gate))
    swapped_upper = lax.ppermute(upper, both, swap)

    relayed = lax.ppermute(crossed, both, [(3, 2), (2, 3), (4, 5), (5, 4)])
    sums, given = call(
        partner_kernel,
        [SDS((1024, 128), F32), SDS((64, 16, 128), BF16)],
        [VMEM] * 4,
        flops=200_000_000, size=3_000_000,
    )(left, crossed, lower, swapped)
    taken = lax.ppermute(given, both, [(0, 3), (1, 2), (7, 4), (6, 5)])

    arrived, given = lax.optimization_barrier((arrived, given))
    opm = call(
        outer_kernel,
        SDS((rows // 2, 128, 128), BF16),
        [VMEM] * 3,
        [
            pltpu.VMEM((64 * MSA_PITCH, 128), F32),
            pltpu.VMEM((32 * MSA_PITCH, 64), F32),
            pltpu.VMEM((64, 2048), BF16),
            pltpu.VMEM((16, 128), F32),
        ],
        flops=1_600_000_000, size=2_000_000,
    )(arrived, wcat, pairwise_final_offset[None])

    return call(
        triangle_kernel,
        SDS((rows, 64, 128), BF16),
        [VMEM] * 14,
        [pltpu.VMEM((128 * SUM_PITCH, 128), F32)],
        flops=400_000_000, size=6_000_000,
    )(
        couple_matrix, upper, swapped_upper, crossed, relayed, left, sums, taken, gate, opm,
        trimul_final_standardize_scaling[None], trimul_final_standardize_offset[None],
        trimul_final_matrix, trimul_final_offset[None],
    )


def solution(mesh):
    placed = (
        P(("crop", "dap"), None, None),
        P(("crop", "dap"), None),
        P(("crop", "dap"), None, None),
        P("crop"),
    ) + (P(),) * 13
    return jax.shard_map(
        local,
        mesh=mesh,
        in_specs=placed,
        out_specs=P(("crop", "dap"), "branch", None),
        check_vma=False,
    )
```

```python
import jax
import jax.numpy as jnp
from jax import lax
from jax.experimental import pallas as pl
from jax.experimental.pallas import tpu as pltpu
from jax.sharding import PartitionSpec as P

F32 = jnp.float32
BF16 = jnp.bfloat16
EPS = 1e-05
NT = (((1,), (1,)), ((), ()))
VMEM = pl.BlockSpec(memory_space=pltpu.VMEM)
SMEM = pl.BlockSpec(memory_space=pltpu.SMEM)
HBM = pl.BlockSpec(memory_space=pltpu.HBM)
ENTRY_MIB = 56
BLOCK = 32
SIDE_PITCH = 132
SUM_PITCH = 24
MSA_PITCH = 40
PAIRS = 16


def dot(a, b):
    return jnp.dot(a, b, preferred_element_type=F32)


def dot_nt(a, b):
    return lax.dot_general(a, b, NT, preferred_element_type=F32)


def sigmoid(v):
    return 0.5 * jnp.tanh(0.5 * v) + 0.5


def flipped(a):
    return jnp.transpose(a.astype(F32))


def column(row, width):
    return jnp.transpose(jnp.broadcast_to(row, (width, row.shape[1])))


def centring(width, copies):
    n = width * copies
    r = lax.broadcasted_iota(jnp.int32, (n, n), 0)
    c = lax.broadcasted_iota(jnp.int32, (n, n), 1)
    inside = (r // width) == (c // width)
    value = jnp.where(r == c, 1.0 - 1.0 / width, -1.0 / width)
    return jnp.where(inside, value, 0.0).astype(BF16)


def deviations(blocks, centre, gain, ones):
    n = len(blocks)
    wide = [jnp.concatenate(blocks[i : i + 2], axis=1) for i in range(0, n, 2)]
    delta = dot(jnp.concatenate(wide, axis=0), centre)
    square = (delta * delta).astype(BF16)
    gained = (delta * jnp.concatenate([gain] * 2, axis=1)).astype(BF16)

    def stacked(a):
        parts = [a[64 * i : 64 * i + 128] if i % 2 == 0 else a[64 * i - 64 : 64 * i + 64] for i in range(n)]
        parts = [p[:, 128 * (i % 2) : 128 * (i % 2) + 128] for i, p in enumerate(parts)]
        return jnp.concatenate(parts, axis=0)

    spread = dot_nt(ones, stacked(square))
    return stacked(gained), lax.rsqrt(spread + EPS)[0:1]


def gate_weights(w_ref, wb_ref, bias, at):
    wt = flipped(w_ref[:, at : at + 256])
    shift = jnp.sum(wt * bias, axis=1, keepdims=True)
    rows = [wb_ref[k : k + 1, :] for k in (at // 128, at // 128 + 1)]
    col = column(jnp.concatenate(rows, axis=1), 128) + shift
    half = jnp.where(lax.broadcasted_iota(jnp.int32, (256, 128), 0) < 128, 0.5, 1.0)
    col = col * half
    return (wt * half).astype(BF16), jnp.concatenate([col, col], axis=1)


def gated(wt, col, gained, scale, live):
    projected = dot_nt(wt, gained) * scale + col
    value = projected[128:256] * live
    return jnp.tanh(projected[0:128]) * value + value


def project_rows(x_ref, present, at, rows, live_k, centre, gain, ones, sides):
    def some(u, _):
        i = BLOCK * u
        gained, scale = deviations([x_ref[i + h] for h in range(BLOCK)], centre, gain, ones)
        for v in range(0, BLOCK, 2):
            live = jnp.concatenate(
                [live_k * (0.5 * present[at + i + v + h].astype(F32)) for h in range(2)], axis=1
            )
            lanes = slice(128 * v, 128 * v + 256)
            for wt, col, scr in sides:
                result = gated(wt, col, gained[lanes], scale[:, lanes], live)
                for h in range(2):
                    scr[pl.ds((i + v + h) * SIDE_PITCH, 128), :] = result[:, 128 * h : 128 * h + 128]
        return 0

    lax.fori_loop(0, rows // BLOCK, some, 0)


def message_part(b, x_ref, flag_ref, window_ref, gain_ref, bias_ref, wt_ref, out_ref):
    seqs, residues, width = x_ref.shape
    ones = jnp.full((8, width), 1.0 / width, BF16)
    centre = centring(width, 1)
    wt = wt_ref[...]
    col = jnp.sum(wt.astype(F32) * bias_ref[...], axis=1, keepdims=True)
    live_all = flag_ref[...].astype(F32) * window_ref[...].astype(F32)
    lane = lax.broadcasted_iota(jnp.int32, (8, 128), 1)
    lane16 = lax.broadcasted_iota(jnp.int32, (16, 128), 1)
    first = b == 0

    delta = dot(x_ref[...].reshape(seqs * residues, width), centre)
    spread = dot_nt(ones, (delta * delta).astype(BF16))
    gained = (delta * gain_ref[...]).astype(BF16)
    everything = dot_nt(wt, gained) * lax.rsqrt(spread + EPS)[0:1] + col
    for s in range(seqs):
        live_row = live_all[s : s + 1, :]
        projected = everything[:, 128 * s : 128 * s + 128] * live_row
        live = jnp.broadcast_to(live_row, (8, 128))
        lo, hi = projected[32:48], projected[48:64]
        right = jnp.where(
            first,
            jnp.where(lane16 < 64, lo, pltpu.roll(hi, 64, 1)),
            jnp.where(lane16 < 64, pltpu.roll(lo, 64, 1), hi),
        )
        live_cols = jnp.where(first, pltpu.roll(live, 32, 1), pltpu.roll(live, 96, 1))
        turned = [[projected[q * 8 : q * 8 + 8]] for q in range(4)]
        for q in range(4):
            turned[q] += [pltpu.roll(turned[q][0], 32 * k, 1) for k in range(1, 4)]
        for dest in range(4):
            merged = turned[0][-dest % 4]
            for q in range(1, 4):
                merged = jnp.where(lane >= 32 * q, turned[q][(q - dest) % 4], merged)
            live_rows = pltpu.roll(live, 128 - 32 * dest, 1) if dest else live
            flags = jnp.where(lane < 32, live_rows, live_cols)
            out_ref[dest, s] = jnp.concatenate([merged, right, flags], axis=0).astype(BF16)


def member_of_half():
    return (lax.axis_index("dap") // 2) == lax.axis_index("branch")


def sides_kernel(
    present, couple, window_ref, gain_ref, bias_ref, weight, offset,
    left_ref, right_ref, cross_ref, offset_out,
    couple_v, weight_v, offset_v, left_scr, right_scr, sems,
):
    rows = couple_v.shape[0]
    member = member_of_half()
    copies = [
        pltpu.make_async_copy(src, dst, sems.at[k])
        for k, (src, dst) in enumerate(
            [(weight, weight_v)]
            + [(offset.at[pl.ds(128 * t, 128)], offset_v.at[t]) for t in range(5)]
            + [(couple, couple_v)]
        )
    ]
    for copy in copies:
        copy.start()
    for copy in copies[:-1]:
        copy.wait()
    offset_out[...] = offset_v[...]
    ones = jnp.full((8, 128), 1.0 / 128, BF16)
    bias = bias_ref[...]
    sides = [
        (*gate_weights(weight_v, offset_v, bias, 256 * k), scr)
        for k, scr in enumerate((left_scr, right_scr))
    ]
    copies[-1].wait()
    live_k = window_ref[...].astype(F32)
    project_rows(
        couple_v, present, lax.axis_index("dap") * rows, rows, live_k,
        centring(128, 2), gain_ref[...], ones, sides,
    )

    def turn(c, _):
        left = [left_scr[pl.ds(c + 64 * h, rows, stride=SIDE_PITCH), :].astype(BF16) for h in range(2)]
        right = [right_scr[pl.ds(c + 64 * h, rows, stride=SIDE_PITCH), :].astype(BF16) for h in range(2)]
        for h in range(2):
            left_ref[c + 64 * h] = left[h]
            right_ref[c + 64 * h] = right[h]
        cross_ref[c] = jnp.where(member, right[1], left[0])
        return 0

    lax.fori_loop(0, 64, turn, 0, unroll=8)


def middle_kernel(
    homolog, flag, window, m_gain, m_bias, m_weight,
    x_ref, gain_ref, bias_ref, w_ref, wb_ref, wf_ref, message_ref, gate_ref, wcat_ref, wf_scr,
):
    b = lax.axis_index("branch")
    message_part(b, homolog, flag, window, m_gain, m_bias, m_weight, message_ref)
    rows = x_ref.shape[0]
    ones = jnp.full((8, 128), 1.0 / 128, BF16)
    centre, gain = centring(128, 2), gain_ref[...]
    wg = flipped(w_ref[:, 512:640])
    gcol = column(wb_ref[4:5, :], 128) + jnp.sum(wg * bias_ref[...], axis=1, keepdims=True)
    wg, gcol = (0.5 * wg).astype(BF16), 0.5 * gcol
    at = pl.multiple_of(64 * b, 64)

    blocks = [
        jnp.concatenate([x_ref[p, pl.ds(at, 64), :], x_ref[p + rows // 2, pl.ds(at, 64), :]], axis=0)
        for p in range(rows // 2)
    ]
    gained, scale = deviations(blocks, centre, gain, ones)
    projected = dot_nt(wg, gained) * scale
    for p in range(rows // 2):
        part = projected[:, 128 * p : 128 * p + 128] + gcol
        gate_ref[p] = 0.5 * jnp.tanh(part) + 0.5

    for c in range(32):
        wf_scr[pl.ds(c * MSA_PITCH, 32), :] = wf_ref[pl.ds(c * 32, 32), :].astype(F32)
    for p in range(2):
        for t in range(4):
            parts = [wf_scr[pl.ds(p * 16 + 4 * t + u, 32, stride=MSA_PITCH), :] for u in range(4)]
            block = jnp.transpose(jnp.concatenate(parts, axis=0))
            wcat_ref[128 * p : 128 * p + 128, 128 * t : 128 * t + 128] = block.astype(BF16)


def outer_kernel(m_ref, wcat_ref, fb_ref, out_ref, m_scr, a_scr, r_scr, inv_scr):
    for k in range(64):
        m_scr[pl.ds(k * MSA_PITCH, 32), :] = m_ref[k // 16, k % 16].astype(F32)

    def row(k):
        return m_scr[pl.ds(k, 64, stride=MSA_PITCH), :]

    flags = row(24)
    count = dot(jnp.transpose(flags).astype(BF16), flags.astype(BF16))[0:32]
    inverse = 1.0 / jnp.maximum(count, 1.0)
    lane = lax.broadcasted_iota(jnp.int32, (16, 128), 1)
    inv_scr[...] = jnp.where(
        lane < 64, pltpu.roll(inverse[0:16], 96, 1), pltpu.roll(inverse[16:32], 32, 1)
    )
    for r in range(8):
        turned = jnp.transpose(row(r))
        for q in range(4):
            a_scr[pl.ds((q * 8 + r) * MSA_PITCH, 32), :] = turned[32 * q : 32 * q + 32]
    for t in range(16):
        r_scr[:, 128 * t : 128 * t + 128] = row(8 + t).astype(BF16)

    wcat = wcat_ref[...]
    bcol = column(fb_ref[...], 128)
    lane2 = lax.broadcasted_iota(jnp.int32, (128, 128), 1)

    def some(u, _):
        first = PAIRS * u
        a = [a_scr[pl.ds(first + p + 16 * h, 32, stride=MSA_PITCH), :] for p in range(PAIRS) for h in range(2)]
        products = dot(jnp.concatenate(a, axis=0).astype(BF16), r_scr[...]).astype(BF16)
        for p in range(PAIRS):
            lo, hi = products[64 * p : 64 * p + 32], products[64 * p + 32 : 64 * p + 64]
            tiles = [slice(128 * t, 128 * t + 128) for t in range(16)]
            stacked = [jnp.concatenate([lo[:, t], hi[:, t]], axis=1) for t in tiles]
            update = dot(wcat, jnp.concatenate(stacked, axis=0))
            a0, a1 = update[0:128, 0:128], update[0:128, 128:256]
            b0, b1 = update[128:256, 0:128], update[128:256, 128:256]
            crossed = pltpu.roll(jnp.where(lane2 < 64, a1, b0), 64, 1)
            total = jnp.where(lane2 < 64, a0, b1) + crossed
            out_ref[first + p] = (total * inv_scr[pl.ds(first + p, 1), :] + bcol).astype(BF16)
        return 0

    lax.fori_loop(0, 16 // PAIRS, some, 0)


def partner_kernel(left_ref, cross_ref, right_ref, swap_ref, own_ref, give_ref):
    even = lax.rem(lax.axis_index("dap"), 2) == 0

    def channel(c, _):
        near, far = right_ref[c], swap_ref[c]
        lo, hi = jnp.where(even, near, far), jnp.where(even, far, near)
        rows = jnp.concatenate([left_ref[c], cross_ref[c]], axis=0)
        prod = dot_nt(rows, jnp.concatenate([lo, hi], axis=0))
        own_ref[pl.ds(c * 16, 16), :] = jnp.concatenate([prod[0:16], prod[16:32]], axis=1)
        give_ref[c] = jnp.concatenate([prod[32:48], prod[48:64]], axis=1).astype(BF16)
        return 0

    lax.fori_loop(0, 64, channel, 0, unroll=32)


def triangle_kernel(
    own_ref, right_ref, swap_ref, cross_ref, relay_ref, left_ref, sum_ref, taken_ref, gate_ref, opm_ref,
    fg_ref, fo_ref, wt_ref, tb_ref, out_ref, t_scr,
):
    d, b = lax.axis_index("dap"), lax.axis_index("branch")
    rows = own_ref.shape[0]
    member = member_of_half()
    even = lax.rem(d, 2) == 0

    for c in range(64):
        t_scr[pl.ds(c * SUM_PITCH, 16), :] = jnp.where(
            member, sum_ref[pl.ds(c * 16, 16), :], taken_ref[c].astype(F32)
        )

    def channel(c, _):
        near = jnp.where(member, right_ref[c + 64], relay_ref[c])
        far = jnp.where(member, swap_ref[c + 64], cross_ref[c])
        lo, hi = jnp.where(even, near, far), jnp.where(even, far, near)
        prod = dot_nt(left_ref[c + 64], jnp.concatenate([lo, hi], axis=0))
        sums = jnp.concatenate([prod[0:16], prod[16:32]], axis=1)
        t_scr[pl.ds((c + 64) * SUM_PITCH, 16), :] = sums
        return 0

    lax.fori_loop(0, 64, channel, 0, unroll=32)

    fg = column(fg_ref[...], 128)
    fo = column(fo_ref[...], 128)
    tb = column(tb_ref[...], 128)
    final = flipped(wt_ref[...]).astype(BF16)

    def finish(p, _):
        x = t_scr[pl.ds(p, 128, stride=SUM_PITCH), :]
        mean = jnp.sum(x, axis=0, keepdims=True) * (1.0 / 128)
        delta = x - mean
        spread = jnp.sum(delta * delta, axis=0, keepdims=True) * (1.0 / 128)
        mid = (delta * lax.rsqrt(spread + EPS) * fg + fo).astype(BF16)
        update = (gate_ref[p] * (dot(final, mid) + tb)).astype(BF16)
        total = jnp.transpose(update.astype(F32) + opm_ref[p].astype(F32))
        at = pl.multiple_of(64 * b, 64)
        for h in range(2):
            i = p + h * (rows // 2)
            base = own_ref[i, pl.ds(at, 64), :].astype(F32)
            out_ref[i] = (base + total[64 * h : 64 * h + 64]).astype(BF16)
        return 0

    lax.fori_loop(0, rows // 2, finish, 0, unroll=16)


def call(kernel, shapes, ins, scratch=(), flops=0, size=0, mib=20):
    return pl.pallas_call(
        kernel,
        out_shape=shapes,
        in_specs=ins,
        out_specs=jax.tree.map(lambda _: VMEM, shapes),
        scratch_shapes=list(scratch),
        compiler_params=pltpu.CompilerParams(vmem_limit_bytes=mib * 1024 * 1024),
        cost_estimate=pl.CostEstimate(flops=flops, bytes_accessed=size, transcendentals=0),
    )


SDS = jax.ShapeDtypeStruct


def local(
    homolog_matrix,
    homolog_entry_flags,
    couple_matrix,
    window_amino_flags,
    pairwise_standardize_scaling,
    pairwise_standardize_offset,
    pairwise_factor_matrices,
    pairwise_final_matrix,
    pairwise_final_offset,
    trimul_entry_standardize_scaling,
    trimul_entry_standardize_offset,
    trimul_entry_matrices,
    trimul_entry_offsets,
    trimul_final_standardize_scaling,
    trimul_final_standardize_offset,
    trimul_final_matrix,
    trimul_final_offset,
):
    rows, residues, width = couple_matrix.shape
    seqs = homolog_matrix.shape[0]
    window = window_amino_flags[None, :]
    both = ("branch", "dap")
    block = SDS((128, rows, 128), BF16)
    pair_gain = trimul_entry_standardize_scaling[None]
    pair_bias = trimul_entry_standardize_offset[None]
    scratch = pltpu.VMEM((rows * SIDE_PITCH, 128), F32)
    half = SDS((64, rows, 128), BF16)

    left, right, cross, offsets = call(
        sides_kernel,
        [block, block, half, SDS((8, 128), F32)],
        [SMEM, HBM, VMEM, VMEM, VMEM, HBM, HBM],
        [
            pltpu.VMEM(couple_matrix.shape, BF16), pltpu.VMEM((128, 640), BF16),
            pltpu.VMEM((8, 128), F32), scratch, scratch, pltpu.SemaphoreType.DMA((7,)),
        ],
        flops=600_000_000, size=4_000_000, mib=ENTRY_MIB,
    )(
        window_amino_flags, couple_matrix, window, pair_gain, pair_bias, trimul_entry_matrices,
        trimul_entry_offsets,
    )
    swap = [(0, 1), (1, 0), (7, 6), (6, 7)]
    crossed = lax.ppermute(
        cross, both, [(0, 3), (3, 0), (1, 2), (2, 1), (4, 7), (7, 4), (5, 6), (6, 5)]
    )
    swapped = lax.ppermute(right, both, swap)

    homolog, cross = lax.optimization_barrier((homolog_matrix, cross))
    message, gate, wcat = call(
        middle_kernel,
        [SDS((4, seqs, 32, 128), BF16), SDS((rows // 2, 128, 128), F32), SDS((256, 512), BF16)],
        [VMEM] * 12,
        [pltpu.VMEM((32 * MSA_PITCH, 128), F32)],
        flops=300_000_000, size=5_000_000, mib=ENTRY_MIB,
    )(
        homolog, homolog_entry_flags, window,
        pairwise_standardize_scaling[None], pairwise_standardize_offset[None],
        pairwise_factor_matrices.T,
        couple_matrix, pair_gain, pair_bias, trimul_entry_matrices, offsets, pairwise_final_matrix,
    )
    arrived = lax.all_to_all(message, "dap", 0, 0, tiled=True)

    relayed = lax.ppermute(crossed, both, [(3, 2), (2, 3), (4, 5), (5, 4)])
    sums, given = call(
        partner_kernel,
        [SDS((1024, 128), F32), SDS((64, 16, 128), BF16)],
        [VMEM] * 4,
        flops=200_000_000, size=3_000_000,
    )(left, crossed, right, swapped)
    taken = lax.ppermute(given, both, [(0, 3), (1, 2), (7, 4), (6, 5)])

    arrived, given = lax.optimization_barrier((arrived, given))
    opm = call(
        outer_kernel,
        SDS((rows // 2, 128, 128), BF16),
        [VMEM] * 3,
        [
            pltpu.VMEM((64 * MSA_PITCH, 128), F32),
            pltpu.VMEM((32 * MSA_PITCH, 64), F32),
            pltpu.VMEM((64, 2048), BF16),
            pltpu.VMEM((16, 128), F32),
        ],
        flops=1_600_000_000, size=2_000_000,
    )(arrived, wcat, pairwise_final_offset[None])

    return call(
        triangle_kernel,
        SDS((rows, 64, 128), BF16),
        [VMEM] * 14,
        [pltpu.VMEM((128 * SUM_PITCH, 128), F32)],
        flops=400_000_000, size=6_000_000,
    )(
        couple_matrix, right, swapped, crossed, relayed, left, sums, taken, gate, opm,
        trimul_final_standardize_scaling[None], trimul_final_standardize_offset[None],
        trimul_final_matrix, trimul_final_offset[None],
    )


def solution(mesh):
    placed = (
        P(("crop", "dap"), None, None),
        P(("crop", "dap"), None),
        P(("crop", "dap"), None, None),
        P("crop"),
    ) + (P(),) * 13
    return jax.shard_map(
        local,
        mesh=mesh,
        in_specs=placed,
        out_specs=P(("crop", "dap"), "branch", None),
        check_vma=False,
    )
```
